256 devices in a mesh: section: 4 (over x_hi, core), dp: 64 (over z, y, x_lo).
Axes of the slice: x: 4 (x_hi: 2, x_lo: 2; x = x_hi * 2 + x_lo), y: 4, z: 8, core: 2. Of those that a mesh axis runs over, the one named last changes fastest.
Arguments:
- partials: bfloat16 [4, 256, 64, 1280], P('section', 'dp'), may hold values from -6 to 6
- latents: bfloat16 [256, 64, 1280], P('dp'), may hold values from -6 to 6
- features: bfloat16 [256, 257, 1280], P('dp'), may hold values from -6 to 6
- feature_gain: float32 [1280], replicated, may hold values from 0.1 to 1.9
- latent_gain: float32 [1280], replicated, may hold values from 0.1 to 1.9
- query_weight: bfloat16 [1280, 768], replicated, may hold values from -6 to 6
- kv_weight: bfloat16 [1280, 1536], replicated, may hold values from -6 to 6
- out_weight: bfloat16 [768, 1280], replicated, may hold values from -0.21875 to 0.21875
- sample_of: int32 [64, 4], P('dp'), may hold values from 0 to 1, never falling along the last dimension, each value on 1 to 3 neighbouring positions
- owner: int32 [256, 1], P('dp'), may hold values from 0 to 3; in each aligned block of 4 rows (0 to 3, 4 to 7, ...) at most 2 rows name the same one
Outputs:
- latent_grad: bfloat16 [4, 128, 64, 1280], P('section', 'dp')
- kv_grad: float32 [1280, 1536], P('dp', 'section')
The draws below stay inside these ranges and needn't reach their ends.
Inputs may be any that keep to these rules, and one draw needn't show every extreme that they name: `owner`: in each aligned block of 4 rows (the images of one index of dp) at most 2 rows name one section, a bound that some block reaches. `sample_of`: each row numbers the samples of its images in order, never falling, each sample having 1 to 3 images.
All inputs are finite; a program needn't handle non-finite values.
Results may differ from the reference program's by a relative error of at most 0.015.
The reference program's roundings to bfloat16 on the way count: a program that leaves them out, or rounds other values in their place, can miss the bound.
Values may be sent and summed in bfloat16 or wider, within the bound.
No kernel may reach another device: no remote copies, remote signals or barrier semaphores. Data moves between devices by JAX's collectives and lax.ppermute only.
A program may use at most 64 MiB of HBM per device.

```python
import math
import jax
import jax.numpy as jnp
import numpy as np
from jax import lax

D = 1280
HEAD_DIM = 96
LATENTS = 64
PATCHES = 257
IMG_DEV = 4
INNER = 768
CAP = 2
SAMP_DEV = 2
SECTIONS = 4
IMAGES = 256
N_SECTION = 4
N_DP = 64


def shared_projections(key):
    base = jax.random.fold_in(key, 31)
    key_query, key_keys, key_values = jax.random.split(base, 3)
    query = jax.random.normal(key_query, (D, INNER), jnp.float32) * D ** (-0.5)
    keys = jax.random.normal(key_keys, (D, INNER), jnp.float32) * D ** (-0.5)
    values = jax.random.normal(key_values, (D, INNER), jnp.float32) * D ** (-0.5)
    query = jnp.clip(query, -6.0, 6.0)
    joined = jnp.clip(jnp.concatenate([keys, values], axis=1), -6.0, 6.0)
    return (query, joined)


def draw_query_weight(key, part):
    return shared_projections(key)[0].astype(jnp.bfloat16)


def draw_kv_weight(key, part):
    return shared_projections(key)[1].astype(jnp.bfloat16)


def draw_latents(key, part):
    key_rows = jax.random.fold_in(jax.random.fold_in(key, 57), 0)
    rows = jax.random.normal(key_rows, (IMAGES, LATENTS, D), jnp.float32)
    return jnp.clip(rows, -6.0, 6.0).astype(jnp.bfloat16)


def block_levels(key, extent, cuts, least, top_value):
    factor_of = 1.0
    for position, shards_of in cuts:
        steps = jax.random.uniform(jax.random.fold_in(jax.random.fold_in(key, 6), position), (shards_of,), jnp.float32, least / len(cuts), top_value / len(cuts))
        factor_of = factor_of * jnp.repeat(jnp.exp(steps), extent[position] // shards_of).reshape((-1,) + (1,) * (len(extent) - 1 - position))
    return factor_of


def split_up(amount, total, reach, slope):
    loads = [(1 << 20) // math.isqrt(standing ** slope) + 1 for standing in range(2, amount + 1)]
    rest, counts = total - reach - (amount - 1), [1] * (amount - 1)
    while rest > 0:
        free = [i for i in range(amount - 1) if counts[i] < reach]
        pool, left = sum([loads[i] for i in free]), rest
        for i in free:
            extra = min(reach - counts[i], max(1, left * loads[i] // pool), rest)
            counts[i] = counts[i] + extra
            rest = rest - extra
    return np.array([reach] + counts)


def ragged(own_key, amount, total, most, skew):
    if amount == 2:
        one = jax.random.randint(own_key, (), max(1, total - most), min(most, total - 1) + 1)
        return jnp.stack([one, total - one])
    sizes = jnp.asarray(split_up(amount, total, most, skew), jnp.int32)
    pairs = (amount - 1) // 2
    giver, sink = sizes[1:1 + 2 * pairs:2], sizes[2:2 + 2 * pairs:2]
    room = jnp.minimum(giver - 1, most - sink)
    passed = jax.random.randint(jax.random.fold_in(own_key, 1), (pairs,), 0, 1 << 20) % (room + 1)
    sizes = sizes.at[1:1 + 2 * pairs:2].set(giver - passed).at[2:2 + 2 * pairs:2].set(sink + passed)
    return sizes[jax.random.permutation(jax.random.fold_in(own_key, 2), amount)]


def shared_out(rng, own, number, rows, number_of, top, most, lean):
    order = jax.random.permutation(rng, number_of)
    packed, ordinary = shares(number_of, rows * top, most, lean, True), shares(number_of, rows * top, most, lean, False)
    places = jnp.arange(number_of)

    def named(sizes, offset_by):
        used = int((sizes > 0).sum())
        fixed = max(1, used // 4)
        moved = fixed + (places - fixed + offset_by * (used - fixed)) % max(1, number_of - fixed)
        return jnp.zeros((number_of,), jnp.int32).at[order[jnp.where(places < fixed, places, moved)]].set(jnp.asarray(sizes, jnp.int32))

    sizes = jnp.where(number % 4 == 0, named(packed, number // 4), named(ordinary, number - number // 4 - 1))
    mixed = jax.random.permutation(jax.random.fold_in(own, 3), number_of)
    donor, taker = mixed[0:number_of // 2 * 2:2], mixed[1:number_of // 2 * 2:2]
    room = jnp.minimum(sizes[donor] - 1, most - sizes[taker]) // 2
    room = jnp.where((donor == order[0]) | (taker == order[0]) | (sizes[taker] == 0), 0, jnp.maximum(room, 0))
    moved = jax.random.randint(jax.random.fold_in(own, 4), (number_of // 2,), 0, 1 << 20) % (room + 1)
    sizes = sizes.at[donor].add(-moved).at[taker].add(moved)
    members = jnp.searchsorted(jnp.cumsum(sizes), jnp.arange(rows * top), side="right").astype(jnp.int32)
    table = members.reshape(top, rows).T
    table = table[jax.random.permutation(jax.random.fold_in(own, 1), rows)]
    offset_by = jax.random.randint(jax.random.fold_in(own, 2), (rows, 1), 0, top)
    return jnp.take_along_axis(table, (jnp.arange(top)[None, :] + offset_by) % top, axis=1)


def shares(number_of, total, most, skew, full):
    portions = [(1 << 20) // math.isqrt(grade ** skew) + 1 for grade in range(1, number_of + 1)]
    largest = most if full else min(most, max(-(-total // number_of), total * portions[0] // sum(portions)))
    least = 1 if total - largest >= number_of - 1 else 0
    counts, surplus = [largest] + [least] * (number_of - 1), total - largest - least * (number_of - 1)
    while surplus > 0:
        candidates = [i for i in range(1, number_of) if counts[i] < largest] or [i for i in range(1, number_of) if counts[i] < most]
        pool, left = sum([portions[i] for i in candidates]), surplus
        for i in candidates:
            more = min(most - counts[i], max(1, left * portions[i] // pool), surplus)
            counts[i] = counts[i] + more
            surplus = surplus - more
    return np.array(counts)


def bell_draw(key, dims, spread, bound, cuts=(), kind=jnp.bfloat16):
    result = jax.random.normal(key, dims, jnp.float32) * spread
    if len(cuts) > 0:
        result = block_levels(key, dims, cuts, -0.22, 0.18) * result
    return jnp.clip(result, min=-bound, max=bound).astype(kind)


def setup_inputs(seed: int = 0) -> dict:
    streams_of = jax.random.split(jax.random.key(seed), 11)
    partials = bell_draw(streams_of[0], (SECTIONS, IMAGES, LATENTS, D), 1.0, 6.0, ((0, 4), (1, 64)))
    latents = draw_latents(jax.random.fold_in(streams_of[10], 71), 0)
    features = bell_draw(streams_of[2], (IMAGES, PATCHES, D), 1.0, 6.0, ((0, 64),))
    feature_gain = jnp.clip(1.0 + 0.18 * jax.random.normal(streams_of[3], (D,), jnp.float32), 0.1, 1.9)
    latent_gain = jnp.clip(1.0 + 0.18 * jax.random.normal(streams_of[4], (D,), jnp.float32), 0.1, 1.9)
    query_weight = draw_query_weight(jax.random.fold_in(streams_of[10], 71), 0)
    kv_weight = draw_kv_weight(jax.random.fold_in(streams_of[10], 71), 0)
    out_weight = bell_draw(streams_of[7], (INNER, D), INNER ** -0.5, 0.21875)
    sample_of = jax.vmap(lambda own: jnp.searchsorted(jnp.cumsum(ragged(own, SAMP_DEV, IMG_DEV, 3, 1)), jnp.arange(IMG_DEV), side="right"))(jax.random.split(streams_of[8], N_DP)).reshape((N_DP, IMG_DEV)).astype(jnp.int32)
    owner_keys = jax.random.split(jax.random.fold_in(streams_of[9], 1), IMAGES // IMG_DEV)
    owner_turns = jax.random.permutation(jax.random.fold_in(streams_of[9], 3), IMAGES // IMG_DEV)
    owner = jax.vmap(lambda own, number: shared_out(jax.random.fold_in(streams_of[9], 2), own, number, IMG_DEV, N_SECTION, 1, CAP, 2))(owner_keys, owner_turns).reshape((IMAGES, 1))
    return {"partials": partials, "latents": latents, "features": features, "feature_gain": feature_gain, "latent_gain": latent_gain, "query_weight": query_weight, "kv_weight": kv_weight, "out_weight": out_weight, "sample_of": sample_of, "owner": owner}


norm_epsilon = 1e-05

def product(form, left, right):
    return jnp.einsum(form, left.astype(jnp.float32), right.astype(jnp.float32))

def layer_stats(values):
    centred = values - lax.optimization_barrier(jnp.mean(values, axis=-1, keepdims=True))
    inverse = lax.rsqrt(lax.optimization_barrier(jnp.mean(centred * centred, axis=-1, keepdims=True)) + norm_epsilon)
    return (centred * inverse, inverse)

def resampler_backward(upstream, latent_rows, patch_rows, feature_gain, latent_gain, query_weight, kv_weight, out_weight):
    count = upstream.shape[0]
    patches = patch_rows.shape[1]
    latent_count = latent_rows.shape[1]
    inner_width = query_weight.shape[1]
    heads_total = inner_width // HEAD_DIM
    factor = HEAD_DIM ** (-0.5)
    patch_hat, _ = layer_stats(patch_rows.astype(jnp.float32))
    normed_patches = (patch_hat * feature_gain).astype(jnp.bfloat16)
    latent_hat, latent_inverse = layer_stats(latent_rows.astype(jnp.float32))
    normed_latents = (latent_hat * latent_gain).astype(jnp.bfloat16)
    context = jnp.concatenate([normed_patches, normed_latents], axis=1)
    context_len = patches + latent_count
    queries = product('nld,de->nle', normed_latents, query_weight).astype(jnp.bfloat16)
    keyvals = product('ncd,de->nce', context, kv_weight).astype(jnp.bfloat16)
    query_heads = queries.reshape(count, latent_count, heads_total, HEAD_DIM)
    key_heads = keyvals[..., :inner_width].reshape(count, context_len, heads_total, HEAD_DIM)
    value_heads = keyvals[..., inner_width:].reshape(count, context_len, heads_total, HEAD_DIM)
    scores = product('nqhd,nkhd->nhqk', query_heads, key_heads) * factor
    shifted = jnp.exp(scores - lax.optimization_barrier(jnp.max(scores, axis=-1, keepdims=True)))
    probs = shifted / lax.optimization_barrier(jnp.sum(shifted, axis=-1, keepdims=True))
    probs_low = probs.astype(jnp.bfloat16)
    attn_grad = product('nld,ed->nle', upstream, out_weight).astype(jnp.bfloat16)
    attn_heads = attn_grad.reshape(count, latent_count, heads_total, HEAD_DIM)
    prob_grad = product('nqhd,nkhd->nhqk', attn_heads, value_heads)
    value_grad = product('nhqk,nqhd->nkhd', probs_low, attn_heads)
    score_grad = (probs * (prob_grad - lax.optimization_barrier(jnp.sum(probs * prob_grad, axis=-1, keepdims=True))) * factor).astype(jnp.bfloat16)
    query_grad = product('nhqk,nkhd->nqhd', score_grad, key_heads).astype(jnp.bfloat16).reshape(count, latent_count, inner_width)
    key_grad = product('nhqk,nqhd->nkhd', score_grad, query_heads).reshape(count, context_len, inner_width)
    keyval_grad = jnp.concatenate([key_grad, value_grad.reshape(count, context_len, inner_width)], axis=-1).astype(jnp.bfloat16)
    weight_term = product('ncd,nce->de', context, keyval_grad)
    normed_grad = product('nle,de->nld', query_grad, query_weight) + product('nle,de->nld', keyval_grad[:, patches:], kv_weight)
    dy_rows = normed_grad * latent_gain
    centred = dy_rows - lax.optimization_barrier(jnp.mean(dy_rows, axis=-1, keepdims=True)) - latent_hat * lax.optimization_barrier(jnp.mean(dy_rows * latent_hat, axis=-1, keepdims=True))
    image_grad = (upstream.astype(jnp.float32) + latent_inverse * centred).astype(jnp.bfloat16)
    return (image_grad, weight_term)

def reference(partials, latents, features, feature_gain, latent_gain, query_weight, kv_weight, out_weight, sample_of, owner):
    summed = lax.optimization_barrier(jnp.sum(partials.astype(jnp.float32), axis=0))
    same = (sample_of[:, :, None] == sample_of[:, None, :]).astype(jnp.float32)
    scale = (1.0 / lax.optimization_barrier(jnp.sum(same, axis=-1))).reshape(IMAGES)
    upstream = (summed * scale[:, None, None]).astype(jnp.bfloat16)

    def block_step(total, block):
        up_rows, lat_rows, feat_rows = block
        image_grad, weight_term = resampler_backward(up_rows, lat_rows, feat_rows, feature_gain, latent_gain, query_weight, kv_weight, out_weight)
        return (total + weight_term, image_grad)
    total, image_grads = lax.scan(block_step, jnp.zeros((D, 2 * INNER), jnp.float32), (upstream.reshape(N_DP, IMG_DEV, LATENTS, D), latents.reshape(N_DP, IMG_DEV, LATENTS, D), features.reshape(N_DP, IMG_DEV, PATCHES, D)))
    owners = owner.reshape(N_DP, IMG_DEV)
    positions = jnp.arange(IMG_DEV, dtype=jnp.int32)
    before = (owners[:, :, None] == owners[:, None, :]) & (positions[None, None, :] < positions[None, :, None])
    ranking = lax.optimization_barrier(jnp.sum(before.astype(jnp.int32), axis=-1))
    section_ids = jnp.arange(SECTIONS, dtype=jnp.int32)
    slot_ids = jnp.arange(CAP, dtype=jnp.int32)
    placing = ((owners[:, None, None, :] == section_ids[None, :, None, None]) & (ranking[:, None, None, :] == slot_ids[None, None, :, None])).astype(jnp.float32)
    slotted = jnp.einsum('psci,pild->spcld', placing, image_grads.astype(jnp.float32))
    latent_grad = slotted.reshape(SECTIONS, N_DP * CAP, LATENTS, D).astype(jnp.bfloat16)
    return (latent_grad, total / IMAGES)
```

```python
import functools
import jax
import jax.numpy as jnp
from jax import lax
from jax.experimental import pallas as pl
from jax.experimental.pallas import tpu as pltpu
from jax.sharding import Mesh, PartitionSpec as P

HEAD = 96
IMGS = 4
LAT = 64
PATCH = 257
TOK = 321
ROWS = 336
D = 1280
INNER = 768
EPS = 1e-05
BF = jnp.bfloat16
F32 = jnp.float32
FACTOR = HEAD ** (-0.5)
SHARE = 20


def dot(a, b, ca, cb):
    return lax.dot_general(a, b, (((ca,), (cb,)), ((), ())), preferred_element_type=F32)


def pair_of(xh, co):
    return co * 2 + xh


def window_of(pair):
    return (pair // 2) * 384 + (pair % 2) * 128


def spread(pair):
    src = lax.broadcasted_iota(jnp.int32, (256, 256), 0)
    dst = lax.broadcasted_iota(jnp.int32, (256, 256), 1)
    lane = dst % 128
    hit = (lane < HEAD) & (src == (pair % 2) * 64 + (dst // 128) * HEAD + lane)
    return jnp.where(hit, 1.0, 0.0).astype(BF)


def layer_stats(x):
    centred = x - jnp.mean(x, axis=-1, keepdims=True)
    inverse = lax.rsqrt(jnp.mean(centred * centred, axis=-1, keepdims=True) + EPS)
    return centred * inverse, inverse


def slot_image(owner_ref, section, slot):
    found = jnp.int32(0)
    index = jnp.int32(0)
    seen = jnp.int32(0)
    for i in range(IMGS):
        mine = (owner_ref[i, 0] == section).astype(jnp.int32)
        take = (mine == 1) & (seen == slot)
        index = jnp.where(take, i, index)
        found = jnp.where(take, 1, found)
        seen = seen + mine
    return index, found


def scale_of(sample_ref, i):
    count = jnp.int32(0)
    for k in range(IMGS):
        count = count + (sample_ref[0, k] == sample_ref[0, i]).astype(jnp.int32)
    return count


def attn_kernel(owner_ref, part_ref, ow_ref, a0, a1, a2, a3, u1, u2, u3, prod):
    xh = lax.axis_index("xh")
    co = lax.axis_index("co")
    rows = part_ref[...].reshape(IMGS * LAT, D)
    prod[...] = dot(rows, ow_ref[...], 1, 1).astype(BF)
    for out, (dx, dc) in zip((a0, a1, a2, a3), ((0, 0), (0, 1), (1, 0), (1, 1))):
        pair = pair_of(xh ^ dx, co ^ dc)
        start = pl.multiple_of(window_of(pair), 128)
        out[...] = dot(prod[:, pl.ds(start, 256)], spread(pair), 1, 0).astype(BF)
    for out, (dx, dc) in zip((u1, u2, u3), ((0, 1), (1, 0), (1, 1))):
        section = (xh ^ dx) * 2 + (co ^ dc)
        for slot in range(2):
            index, _ = slot_image(owner_ref, section, slot)
            out[slot] = part_ref[index]


def forward_kernel(feat_ref, lat_ref, fg_ref, lg_ref, qw_hbm, kvw_hbm, ctx_ref, kv_ref, q_ref, pr_ref,
                   win, wp, sems):
    i = pl.program_id(0)

    @pl.when(i == 0)
    def _():
        xh = lax.axis_index("xh")
        co = lax.axis_index("co")
        pair = pair_of(xh, co)
        start = pl.multiple_of(window_of(pair), 128)
        copies = [
            pltpu.make_async_copy(qw_hbm.at[:, pl.ds(start, 256)], win.at[0], sems.at[0]),
            pltpu.make_async_copy(kvw_hbm.at[:, pl.ds(start, 256)], win.at[1], sems.at[1]),
            pltpu.make_async_copy(kvw_hbm.at[:, pl.ds(pl.multiple_of(start + INNER, 128), 256)], win.at[2], sems.at[2]),
        ]
        for c in copies:
            c.start()
        table = spread(pair)
        for k, c in enumerate(copies):
            c.wait()
            wp[:, 256 * k:256 * (k + 1)] = dot(win[k], table, 1, 0).astype(BF)

    patch_hat, _ = layer_stats(feat_ref[0].astype(F32))
    lat_hat, _ = layer_stats(lat_ref[0].astype(F32))
    normed = (lat_hat * lg_ref[...]).astype(BF)
    ctx_ref[0, 320:ROWS] = jnp.zeros((ROWS - 320, D), BF)
    ctx_ref[0, LAT:TOK] = (patch_hat * fg_ref[...]).astype(BF)
    ctx_ref[0, 0:LAT] = normed
    kv_ref[0] = dot(ctx_ref[0], wp[:, 256:], 1, 0).astype(BF)
    q_ref[0] = dot(normed, wp[:, :256], 1, 0).astype(BF)
    live = lax.broadcasted_iota(jnp.int32, (LAT, ROWS), 1) < TOK
    for h in range(2):
        lanes = slice(128 * h, 128 * (h + 1))
        scores = dot(q_ref[0, :, lanes], kv_ref[0, :, lanes], 1, 1) * FACTOR
        scores = jnp.where(live, scores, -1e30)
        shifted = jnp.exp(scores - jnp.max(scores, axis=-1, keepdims=True))
        shifted = jnp.where(live, shifted, 0.0)
        pr_ref[0, h] = shifted / jnp.sum(shifted, axis=-1, keepdims=True)


def backward_kernel(owner_ref, sample_ref, a0, a1, a2, a3, ctx_ref, kv_ref, q_ref, pr_ref,
                    w_ref, g0, g1, g2, g3, kvg, wide, order, lat):
    xh = lax.axis_index("xh")
    co = lax.axis_index("co")
    for i in range(IMGS):
        rows = slice(LAT * i, LAT * (i + 1))
        count = scale_of(sample_ref, i).astype(F32)
        total = (a0[rows].astype(F32) + a1[rows].astype(F32)) + (a2[rows].astype(F32) + a3[rows].astype(F32))
        attn = (total / count).astype(BF)
        grads = []
        for h in range(2):
            lanes = slice(128 * h, 128 * (h + 1))
            vlanes = slice(256 + 128 * h, 256 + 128 * (h + 1))
            probs = pr_ref[i, h]
            a = attn[:, lanes]
            value_grad = dot(probs.astype(BF), a, 0, 0)
            prob_grad = dot(a, kv_ref[i, :, vlanes], 1, 1)
            inner = jnp.sum(probs * prob_grad, axis=-1, keepdims=True)
            score_grad = (probs * (prob_grad - inner) * FACTOR).astype(BF)
            query_grad = dot(score_grad, kv_ref[i, :, lanes], 1, 0)
            key_grad = dot(score_grad, q_ref[i, :, lanes], 0, 0)
            lat[rows, lanes] = query_grad.astype(BF)
            lat[rows, 256 + 128 * h:256 + 128 * (h + 1)] = key_grad[:LAT].astype(BF)
            lat[rows, 512 + 128 * h:512 + 128 * (h + 1)] = value_grad[:LAT].astype(BF)
            grads.append((key_grad[:, :HEAD], value_grad[:, :HEAD]))
        kvg[ROWS * i:ROWS * (i + 1)] = jnp.concatenate(
            [grads[0][0], grads[1][0], grads[0][1], grads[1][1]], axis=1).astype(BF)
    table = spread(pair_of(xh, co))
    for k in range(3):
        lanes = slice(256 * k, 256 * (k + 1))
        lat[:, lanes] = dot(lat[:, lanes], table, 1, 1).astype(BF)
    for out, (dx, dc) in zip((g0, g1, g2, g3), ((0, 0), (0, 1), (1, 0), (1, 1))):
        section = (xh ^ dx) * 2 + (co ^ dc)
        for slot in range(2):
            index, _ = slot_image(owner_ref, section, slot)
            out[LAT * slot:LAT * (slot + 1)] = lat[pl.ds(pl.multiple_of(index * LAT, LAT), LAT)]
    ctx = ctx_ref[...].reshape(IMGS * ROWS, D)
    for c in range(5):
        wide[256 * c:256 * (c + 1)] = dot(ctx[:, 256 * c:256 * (c + 1)], kvg[...], 0, 0)
    for y in range(4):
        for xl in range(2):
            piece = xl * 4 + y
            for z in range(8):
                first = ((z * 4 + y) * 2 + xl) * SHARE
                block = wide[first:first + SHARE]
                to = z * SHARE
                order[piece, to:to + SHARE, :] = block
            whole = order[piece]
            keys = whole[:, :128], whole[:, 128:192]
            vals = whole[:, 256:], whole[:, 192:256]
            for k, (main, tail) in enumerate((keys, vals)):
                w_ref[8 * k + piece, 0:160] = main.astype(BF)
                w_ref[8 * k + piece, 160:240] = jnp.concatenate([tail[:80], tail[80:]], axis=1).astype(BF)


def first_sum_kernel(r_ref, out_ref, full):
    halves = []
    for k in range(2):
        total = r_ref[8 * k].astype(F32)
        for p in range(1, 8):
            total = total + r_ref[8 * k + p].astype(F32)
        main, tail = total[:160], total[160:]
        tail = jnp.concatenate([tail[:, :64], tail[:, 64:]], axis=0)
        halves.append((main, tail))
    return halves


def stage_kernel(r_ref, out_ref, full):
    here = lax.axis_index("xh")
    halves = first_sum_kernel(r_ref, out_ref, full)

    @pl.when(here == 0)
    def _():
        for k, (main, tail) in enumerate(halves):
            full[:, 192 * k:192 * (k + 1)] = jnp.concatenate([main, tail], axis=1)

    @pl.when(here == 1)
    def _():
        for k, (main, tail) in enumerate(halves):
            full[:, 192 * k:192 * (k + 1)] = jnp.concatenate([tail, main], axis=1)

    for z in range(8):
        out_ref[z, 0:SHARE] = full[SHARE * z:SHARE * (z + 1)].astype(BF)


def last_kernel(r_ref, out_ref):
    total = r_ref[0].astype(F32)
    for z in range(1, 8):
        total = total + r_ref[z].astype(F32)
    out_ref[...] = total[:SHARE] * (1.0 / 256.0)


def latent_kernel(owner_ref, sample_ref, part_ref, lat_ref, lg_ref, qw_ref, kvw_ref,
                  u1, u2, u3, g0, g1, g2, g3, out_ref):
    xh = lax.axis_index("xh")
    co = lax.axis_index("co")
    section = xh * 2 + co
    grad = jnp.zeros((2 * LAT, D), F32)
    for g, (dx, dc) in zip((g0, g1, g2, g3), ((0, 0), (0, 1), (1, 0), (1, 1))):
        start = pl.multiple_of(window_of(pair_of(xh ^ dx, co ^ dc)), 128)
        grad = grad + dot(g[:, 0:256], qw_ref[:, pl.ds(start, 256)], 1, 1)
        grad = grad + dot(g[:, 256:512], kvw_ref[:, pl.ds(start, 256)], 1, 1)
        grad = grad + dot(g[:, 512:768], kvw_ref[:, pl.ds(pl.multiple_of(start + INNER, 128), 256)], 1, 1)
    for slot in range(2):
        index, found = slot_image(owner_ref, section, slot)
        count = scale_of(sample_ref, index).astype(F32)
        summed = (part_ref[index].astype(F32) + u1[slot].astype(F32)) + (u2[slot].astype(F32) + u3[slot].astype(F32))
        upstream = (summed / count).astype(BF).astype(F32)
        hat, inverse = layer_stats(lat_ref[index].astype(F32))
        dy = grad[LAT * slot:LAT * (slot + 1)] * lg_ref[...]
        centred = dy - jnp.mean(dy, axis=-1, keepdims=True) - hat * jnp.mean(dy * hat, axis=-1, keepdims=True)
        out = (upstream + inverse * centred).astype(BF)
        out_ref[slot] = jnp.where(found == 1, out, jnp.zeros_like(out))


def call(body, outs, ins, scratch, flops=0, size=0, limit=40, grid=None, name=None):
    vm = pl.BlockSpec(memory_space=pltpu.VMEM)
    return pl.pallas_call(
        body,
        out_shape=outs,
        in_specs=ins,
        out_specs=jax.tree.map(lambda _: vm, outs),
        scratch_shapes=scratch,
        cost_estimate=pl.CostEstimate(flops=flops, bytes_accessed=size, transcendentals=0),
        compiler_params=pltpu.CompilerParams(vmem_limit_bytes=limit * 2**20),
        name=name,
    )


SMEM = pl.BlockSpec(memory_space=pltpu.SMEM)
VMEM = pl.BlockSpec(memory_space=pltpu.VMEM)
CORE = [(0, 1), (1, 0), (2, 3), (3, 2)]
FAR = [(0, 2), (2, 0), (1, 3), (3, 1)]
DIAGONAL = [(0, 3), (3, 0), (1, 2), (2, 1)]
SECTION = ("xh", "co")


def swap(x, pairs):
    return lax.ppermute(x, SECTION, pairs)


def per_device(partials, latents, features, feature_gain, latent_gain, query_weight, kv_weight, out_weight,
               sample_of, owner):
    part = partials[0]
    fg = feature_gain.reshape(1, D)
    lg = latent_gain.reshape(1, D)
    sd = jax.ShapeDtypeStruct
    a0, a1, a2, a3, u1, u2, u3 = call(
        attn_kernel,
        [sd((256, 256), BF)] * 4 + [sd((2, LAT, D), BF)] * 3,
        [SMEM, VMEM, VMEM],
        [pltpu.VMEM((256, INNER), BF)],
        flops=600_000_000, size=3_000_000, name="attn_part",
    )(owner, part, out_weight)
    a3 = swap(a3, DIAGONAL)
    a2 = swap(a2, FAR)
    a1 = swap(a1, CORE)
    whole = lambda *shape: pl.BlockSpec(shape, lambda i: (0,) * len(shape))
    image = lambda *shape: pl.BlockSpec((1,) + shape, lambda i: (i,) + (0,) * len(shape))
    ctx, kv, q, probs = pl.pallas_call(
        forward_kernel,
        grid=(IMGS,),
        out_shape=[sd((IMGS, ROWS, D), BF), sd((IMGS, ROWS, 512), BF), sd((IMGS, LAT, 256), BF),
                   sd((IMGS, 2, LAT, ROWS), F32)],
        in_specs=[image(PATCH, D), image(LAT, D), whole(1, D), whole(1, D),
                  pl.BlockSpec(memory_space=pl.ANY), pl.BlockSpec(memory_space=pl.ANY)],
        out_specs=[image(ROWS, D), image(ROWS, 512), image(LAT, 256), image(2, LAT, ROWS)],
        scratch_shapes=[pltpu.VMEM((3, D, 256), BF), pltpu.VMEM((D, 768), BF), pltpu.SemaphoreType.DMA((3,))],
        cost_estimate=pl.CostEstimate(flops=4_000_000_000, bytes_accessed=12_000_000, transcendentals=0),
        compiler_params=pltpu.CompilerParams(vmem_limit_bytes=40 * 2**20),
        name="forward_part",
    )(features, latents, fg, lg, query_weight, kv_weight)
    w, g0, g1, g2, g3 = call(
        backward_kernel,
        [sd((16, 240, 128), BF)] + [sd((2 * LAT, 768), BF)] * 4,
        [SMEM, SMEM] + [VMEM] * 8,
        [pltpu.VMEM((IMGS * ROWS, 384), BF), pltpu.VMEM((D, 384), F32), pltpu.VMEM((8, 160, 384), F32),
         pltpu.VMEM((256, 768), BF)],
        flops=4_000_000_000, size=10_000_000, name="backward_part",
    )(owner, sample_of, a0, a1, a2, a3, ctx, kv, q, probs)
    w = lax.all_to_all(w, ("xh", "xl", "y"), 0, 0, tiled=True)
    w = call(stage_kernel, sd((8, 32, 384), BF), [VMEM], [pltpu.VMEM((160, 384), F32)],
             size=1_000_000, name="first_sum")(w)
    u3 = swap(u3, DIAGONAL)
    u2 = swap(u2, FAR)
    u1 = swap(u1, CORE)
    g3 = swap(g3, DIAGONAL)
    g2 = swap(g2, FAR)
    g1 = swap(g1, CORE)
    w = lax.all_to_all(w, "z", 0, 0, tiled=True)
    kv_grad = call(last_kernel, sd((SHARE, 384), F32), [VMEM], [], size=300_000, name="last_sum")(w)
    latent_grad = call(
        latent_kernel, sd((2, LAT, D), BF), [SMEM, SMEM] + [VMEM] * 12, [],
        flops=1_000_000_000, size=9_000_000, name="latent_part",
    )(owner, sample_of, part, latents, lg, query_weight, kv_weight, u1, u2, u3, g0, g1, g2, g3)
    return latent_grad[None], kv_grad


def solution(mesh):
    fine = Mesh(mesh.devices.reshape(2, 2, 8, 4, 2), ("xh", "co", "z", "y", "xl"))
    dp = ("z", "y", "xl")
    return jax.shard_map(
        per_device,
        mesh=fine,
        in_specs=(
            P(SECTION, dp, None, None),
            P(dp, None, None),
            P(dp, None, None),
            P(),
            P(),
            P(),
            P(),
            P(),
            P(dp, None),
            P(dp, None),
        ),
        out_specs=(P(SECTION, dp, None, None), P(dp, SECTION)),
        check_vma=False,
    )
```

```python
import functools
import jax
import jax.numpy as jnp
from jax import lax
from jax.experimental import pallas as pl
from jax.experimental.pallas import tpu as pltpu
from jax.sharding import Mesh, PartitionSpec as P

HEAD = 96
IMGS = 4
LAT = 64
PATCH = 257
TOK = 321
ROWS = 336
D = 1280
INNER = 768
EPS = 1e-05
BF = jnp.bfloat16
F32 = jnp.float32
FACTOR = HEAD ** (-0.5)
SHARE = 20


def dot(a, b, ca, cb):
    return lax.dot_general(a, b, (((ca,), (cb,)), ((), ())), preferred_element_type=F32)


def pair_of(xh, co):
    return co * 2 + xh


def window_of(pair):
    return (pair // 2) * 384 + (pair % 2) * 128


def head_lanes(pair, head, rows):
    lane = lax.broadcasted_iota(jnp.int32, (rows, 256), 1) - ((pair % 2) * 64 + head * HEAD)
    return (lane >= 0) & (lane < HEAD)


def by_head(x, pair):
    zero = jnp.zeros_like(x)
    return jnp.concatenate([jnp.where(head_lanes(pair, h, x.shape[0]), x, zero) for h in range(2)], axis=0)


def layer_stats(x):
    centred = x - jnp.mean(x, axis=-1, keepdims=True)
    inverse = lax.rsqrt(jnp.mean(centred * centred, axis=-1, keepdims=True) + EPS)
    return centred * inverse, inverse


def slot_image(owner_ref, section, slot):
    found = jnp.int32(0)
    index = jnp.int32(0)
    seen = jnp.int32(0)
    for i in range(IMGS):
        mine = (owner_ref[0, i] == section).astype(jnp.int32)
        take = (mine == 1) & (seen == slot)
        index = jnp.where(take, i, index)
        found = jnp.where(take, 1, found)
        seen = seen + mine
    return index, found


def scale_of(sample_ref, i):
    count = jnp.int32(0)
    for k in range(IMGS):
        count = count + (sample_ref[0, k] == sample_ref[0, i]).astype(jnp.int32)
    return count


AROUND = ((0, 0), (0, 1), (1, 0), (1, 1))


def attn_kernel(part_hbm, ow_hbm, a0, a1, a2, a3, part, wt, prod, sems):
    xh = lax.axis_index("xh")
    co = lax.axis_index("co")
    copies = [pltpu.make_async_copy(part_hbm, part, sems.at[0])]
    for k in range(4):
        rows = pl.ds(192 * k, 192)
        copies.append(pltpu.make_async_copy(ow_hbm.at[rows], wt.at[rows], sems.at[k + 1]))
    for c in copies:
        c.start()
    for c in copies:
        c.wait()
    prod[...] = dot(part[...].reshape(IMGS * LAT, D), wt[...], 1, 1).astype(BF)
    for out, (dx, dc) in zip((a0, a1, a2, a3), AROUND):
        start = pl.multiple_of(window_of(pair_of(xh ^ dx, co ^ dc)), 128)
        out[...] = prod[:, pl.ds(start, 256)]


def chip_sum_kernel(owner_ref, part_ref, c1_ref, u_ref):
    section = (lax.axis_index("xh") ^ 1) * 2 + lax.axis_index("co")
    for slot in range(2):
        index, _ = slot_image(owner_ref, section, slot)
        u_ref[slot] = (part_ref[index].astype(F32) + c1_ref[index].astype(F32)).astype(BF)


def forward_kernel(feat_ref, lat_ref, fg_ref, lg_ref, qw_hbm, kvw_hbm, ctx_ref, kv_ref, q_ref, pr_ref, win, sems):
    pair = pair_of(lax.axis_index("xh"), lax.axis_index("co"))
    start = pl.multiple_of(window_of(pair), 128)
    copies = [
        pltpu.make_async_copy(qw_hbm.at[:, pl.ds(start, 256)], win.at[0], sems.at[0]),
        pltpu.make_async_copy(kvw_hbm.at[:, pl.ds(start, 256)], win.at[1], sems.at[1]),
        pltpu.make_async_copy(kvw_hbm.at[:, pl.ds(pl.multiple_of(start + INNER, 128), 256)], win.at[2], sems.at[2]),
    ]
    for c in copies:
        c.start()
    fg = fg_ref[...].reshape(1, D)
    lg = lg_ref[...].reshape(1, D)
    live = lax.broadcasted_iota(jnp.int32, (2 * LAT, ROWS), 1) < TOK

    def norm(i):
        for c in range(4):
            hat, _ = layer_stats(feat_ref[i, 64 * c:64 * (c + 1)].astype(F32))
            ctx_ref[i, LAT + 64 * c:LAT + 64 * (c + 1)] = (hat * fg).astype(BF)
        hat, _ = layer_stats(lat_ref[i].astype(F32))
        ctx_ref[i, :LAT] = (hat * lg).astype(BF)
        hat, _ = layer_stats(feat_ref[i, 256:257].astype(F32))
        first = lax.broadcasted_iota(jnp.int32, (16, D), 0) == 0
        ctx_ref[i, 320:ROWS] = jnp.where(first, hat * fg, 0.0).astype(BF)

    def project(i):
        kv_ref[i, :, :256] = dot(ctx_ref[i], win[1], 1, 0).astype(BF)
        kv_ref[i, :, 256:] = dot(ctx_ref[i], win[2], 1, 0).astype(BF)
        q_ref[i] = by_head(dot(ctx_ref[i, :LAT], win[0], 1, 0), pair).astype(BF)

    def attend(i):
        scores = dot(q_ref[i], kv_ref[i, :, :256], 1, 1) * FACTOR
        scores = jnp.where(live, scores, -1e30)
        shifted = jnp.exp(scores - jnp.max(scores, axis=-1, keepdims=True))
        shifted = jnp.where(live, shifted, 0.0)
        pr_ref[i] = shifted / jnp.sum(shifted, axis=-1, keepdims=True)

    norm(0)
    for c in copies:
        c.wait()
    for i in range(IMGS):
        if i < IMGS - 1:
            norm(i + 1)
        project(i)
        if i > 0:
            attend(i - 1)
    attend(IMGS - 1)


def backward_kernel(owner_ref, sample_ref, a0, a1, a2, a3, kv_ref, q_ref, pr_ref,
                    kvg, g0, g1, g2, g3, lat):
    xh = lax.axis_index("xh")
    co = lax.axis_index("co")
    pair = pair_of(xh, co)
    left = lax.broadcasted_iota(jnp.int32, (ROWS, 128), 1) < 64
    for i in range(IMGS):
        rows = slice(LAT * i, LAT * (i + 1))
        count = scale_of(sample_ref, i).astype(F32)
        total = (a0[rows].astype(F32) + a1[rows].astype(F32)) + (a2[rows].astype(F32) + a3[rows].astype(F32))
        attn = by_head(total / count, pair).astype(BF)
        probs = pr_ref[i]
        value_grad = dot(probs.astype(BF), attn, 0, 0)
        prob_grad = dot(attn, kv_ref[i, :, 256:], 1, 1)
        inner = jnp.sum(probs * prob_grad, axis=-1, keepdims=True)
        score_grad = (probs * (prob_grad - inner) * FACTOR).astype(BF)
        query_grad = dot(score_grad, kv_ref[i, :, :256], 1, 0)
        query_grad = jnp.where(head_lanes(pair, 0, LAT), query_grad[:LAT],
                               jnp.where(head_lanes(pair, 1, LAT), query_grad[LAT:], 0.0))
        key_grad = dot(score_grad, q_ref[i], 0, 0)
        lat[rows, :256] = query_grad.astype(BF)
        lat[rows, 256:512] = key_grad[:LAT].astype(BF)
        lat[rows, 512:] = value_grad[:LAT].astype(BF)
        at = slice(ROWS * i, ROWS * (i + 1))
        kvg[at, :128] = jnp.where(xh == 0, key_grad[:, :128], key_grad[:, 128:]).astype(BF)
        kvg[at, 128:256] = jnp.where(xh == 0, value_grad[:, :128], value_grad[:, 128:]).astype(BF)
        even = jnp.where(left, key_grad[:, 128:], pltpu.roll(value_grad[:, 128:], 64, 1))
        odd = jnp.where(left, pltpu.roll(key_grad[:, :128], 64, 1), value_grad[:, :128])
        kvg[at, 256:] = jnp.where(xh == 0, even, odd).astype(BF)
    for out, (dx, dc) in zip((g0, g1, g2, g3), AROUND):
        section = (xh ^ dx) * 2 + (co ^ dc)
        for slot in range(2):
            index, _ = slot_image(owner_ref, section, slot)
            out[LAT * slot:LAT * (slot + 1)] = lat[pl.ds(pl.multiple_of(index * LAT, LAT), LAT)]


def weight_kernel(ctx_ref, kvg, w_ref, wide, order):
    ctx = ctx_ref[...].reshape(IMGS * ROWS, D)
    for c in range(5):
        wide[256 * c:256 * (c + 1)] = dot(ctx[:, 256 * c:256 * (c + 1)], kvg[...], 0, 0)
    for y in range(4):
        for xl in range(2):
            piece = xl * 4 + y
            for z in range(8):
                first = ((z * 4 + y) * 2 + xl) * SHARE
                order[piece, z * SHARE:(z + 1) * SHARE] = wide[first:first + SHARE]
            whole = order[piece]
            keys = whole[:, :128], whole[:, 256:320]
            vals = whole[:, 128:256], whole[:, 320:]
            for k, (main, tail) in enumerate((keys, vals)):
                w_ref[8 * k + piece, 0:160] = main.astype(BF)
                w_ref[8 * k + piece, 160:240] = jnp.concatenate([tail[:80], tail[80:]], axis=1).astype(BF)


def first_sum_kernel(r_ref, out_ref, full):
    tails = []
    for k in range(2):
        total = r_ref[8 * k].astype(F32)
        for p in range(1, 8):
            total = total + r_ref[8 * k + p].astype(F32)
        full[:, 256 * k:256 * k + 128] = total[:160]
        tail = total[160:]
        tails.append(jnp.concatenate([tail[:, :64], tail[:, 64:]], axis=0))
    full[:, 128:256] = jnp.concatenate(tails, axis=1)
    for z in range(8):
        out_ref[z, 0:SHARE] = full[SHARE * z:SHARE * (z + 1)].astype(BF)


def last_kernel(r_ref, out_ref):
    total = r_ref[0].astype(F32)
    for z in range(1, 8):
        total = total + r_ref[z].astype(F32)
    out_ref[...] = total[:SHARE] * (1.0 / 256.0)


def latent_kernel(owner_ref, sample_ref, part_ref, lat_ref, lg_ref, qw_hbm, kvw_hbm,
                  c1, u2, g0, g1, g2, g3, out_ref, win, sems):
    xh = lax.axis_index("xh")
    co = lax.axis_index("co")
    section = xh * 2 + co
    copies = []
    for dx, dc in AROUND:
        start = pl.multiple_of(window_of(pair_of(xh ^ dx, co ^ dc)), 128)
        further = pl.multiple_of(start + INNER, 128)
        for k, (source, lane) in enumerate(((qw_hbm, start), (kvw_hbm, start), (kvw_hbm, further))):
            n = len(copies)
            copies.append(pltpu.make_async_copy(source.at[:, pl.ds(lane, 256)], win.at[n], sems.at[n]))
    for c in copies:
        c.start()
    grad = jnp.zeros((2 * LAT, D), F32)
    for n, c in enumerate(copies):
        c.wait()
        k = n % 3
        grad = grad + dot((g0, g1, g2, g3)[n // 3][:, 256 * k:256 * (k + 1)], win[n], 1, 1)
    lg = lg_ref[...].reshape(1, D)
    for slot in range(2):
        index, found = slot_image(owner_ref, section, slot)
        count = scale_of(sample_ref, index).astype(F32)
        summed = (part_ref[index].astype(F32) + c1[index].astype(F32)) + u2[slot].astype(F32)
        upstream = (summed / count).astype(BF).astype(F32)
        hat, inverse = layer_stats(lat_ref[index].astype(F32))
        dy = grad[LAT * slot:LAT * (slot + 1)] * lg
        centred = dy - jnp.mean(dy, axis=-1, keepdims=True) - hat * jnp.mean(dy * hat, axis=-1, keepdims=True)
        out = (upstream + inverse * centred).astype(BF)
        out_ref[slot] = jnp.where(found == 1, out, jnp.zeros_like(out))


SMEM = pl.BlockSpec(memory_space=pltpu.SMEM)
VMEM = pl.BlockSpec(memory_space=pltpu.VMEM)
HBM = pl.BlockSpec(memory_space=pltpu.HBM)
CORE = [(0, 1), (1, 0), (2, 3), (3, 2)]
FAR = [(0, 2), (2, 0), (1, 3), (3, 1)]
DIAGONAL = [(0, 3), (3, 0), (1, 2), (2, 1)]
SECTION = ("xh", "co")


def call(body, name, outs, ins, scratch=(), flops=0, size=0, limit=24):
    return pl.pallas_call(
        body,
        out_shape=outs,
        in_specs=ins,
        out_specs=jax.tree.map(lambda _: VMEM, outs),
        scratch_shapes=list(scratch),
        cost_estimate=pl.CostEstimate(flops=flops, bytes_accessed=size, transcendentals=0),
        compiler_params=pltpu.CompilerParams(vmem_limit_bytes=limit * 2**20),
        name=name,
    )


def swap(x, pairs):
    return lax.ppermute(x, SECTION, pairs)


def bf(*shape):
    return jax.ShapeDtypeStruct(shape, BF)


DMA = pltpu.SemaphoreType.DMA
CALLS = dict(
    attn=call(
        attn_kernel, "attn_part", [bf(256, 256)] * 4, [HBM] * 2,
        [pltpu.VMEM((IMGS, LAT, D), BF), pltpu.VMEM((INNER, D), BF), pltpu.VMEM((256, INNER), BF), DMA((5,))],
        flops=600_000_000, size=3_000_000, limit=60),
    chip=call(chip_sum_kernel, "chip_sum", bf(2, LAT, D), [SMEM] + [VMEM] * 2, size=1_500_000),
    forward=call(
        forward_kernel, "forward_part",
        [bf(IMGS, ROWS, D), bf(IMGS, ROWS, 512), bf(IMGS, 2 * LAT, 256),
         jax.ShapeDtypeStruct((IMGS, 2 * LAT, ROWS), F32)],
        [VMEM] * 4 + [HBM] * 2,
        [pltpu.VMEM((3, D, 256), BF), DMA((3,))],
        flops=4_000_000_000, size=12_000_000),
    backward=call(
        backward_kernel, "backward_part", [bf(IMGS * ROWS, 384)] + [bf(2 * LAT, 768)] * 4,
        [SMEM, SMEM] + [VMEM] * 7, [pltpu.VMEM((256, 768), BF)],
        flops=2_000_000_000, size=5_000_000),
    weight=call(
        weight_kernel, "weight_part", bf(16, 240, 128), [VMEM] * 2,
        [pltpu.VMEM((D, 384), F32), pltpu.VMEM((8, 160, 384), F32)],
        flops=3_000_000_000, size=6_000_000),
    first=call(first_sum_kernel, "first_sum", bf(8, 32, 384), [VMEM], [pltpu.VMEM((160, 384), F32)],
               size=1_000_000),
    last=call(last_kernel, "last_sum", jax.ShapeDtypeStruct((SHARE, 384), F32), [VMEM], size=300_000),
    latent=call(
        latent_kernel, "latent_part", bf(2, LAT, D), [SMEM, SMEM] + [VMEM] * 3 + [HBM] * 2 + [VMEM] * 6,
        [pltpu.VMEM((12, D, 256), BF), DMA((12,))],
        flops=2_000_000_000, size=9_000_000, limit=60),
)


def per_device(partials, latents, features, feature_gain, latent_gain, query_weight, kv_weight, out_weight,
               sample_of, owner):
    part = partials[0]
    owner = owner.reshape(1, IMGS)
    c1 = swap(part, CORE)
    a0, a1, a2, a3 = CALLS["attn"](part, out_weight)
    a3 = swap(a3, DIAGONAL)
    a2 = swap(a2, FAR)
    a1 = swap(a1, CORE)
    u = swap(CALLS["chip"](owner, part, c1), FAR)
    ctx, kv, q, probs = CALLS["forward"](
        features, latents, feature_gain, latent_gain, query_weight, kv_weight)
    kvg, g0, g1, g2, g3 = CALLS["backward"](owner, sample_of, a0, a1, a2, a3, kv, q, probs)
    kvg, u = lax.optimization_barrier((kvg, u))
    g3 = swap(g3, DIAGONAL)
    g2 = swap(g2, FAR)
    g1 = swap(g1, CORE)
    w = CALLS["weight"](ctx, kvg)
    w, g1, g2, g3 = lax.optimization_barrier((w, g1, g2, g3))
    w = lax.all_to_all(w, ("xh", "xl", "y"), 0, 0, tiled=True)
    w = CALLS["first"](w)
    latent_grad = CALLS["latent"](
        owner, sample_of, part, latents, latent_gain, query_weight, kv_weight, c1, u, g0, g1, g2, g3)
    w, latent_grad = lax.optimization_barrier((w, latent_grad))
    w = lax.all_to_all(w, "z", 0, 0, tiled=True)
    kv_grad = CALLS["last"](w)
    return latent_grad[None], kv_grad


def solution(mesh):
    fine = Mesh(mesh.devices.reshape(2, 2, 8, 4, 2), ("xh", "co", "z", "y", "xl"))
    dp = ("z", "y", "xl")
    return jax.shard_map(
        per_device,
        mesh=fine,
        in_specs=(
            P(SECTION, dp, None, None),
            P(dp, None, None),
            P(dp, None, None),
            P(),
            P(),
            P(),
            P(),
            P(),
            P(dp, None),
            P(dp, None),
        ),
        out_specs=(P(SECTION, dp, None, None), P(dp, SECTION)),
        check_vma=False,
    )
```

```python
import functools
import jax
import jax.numpy as jnp
from jax import lax
from jax.experimental import pallas as pl
from jax.experimental.pallas import tpu as pltpu
from jax.sharding import Mesh, PartitionSpec as P

HEAD = 96
IMGS = 4
LAT = 64
PATCH = 257
TOK = 321
ROWS = 336
D = 1280
INNER = 768
EPS = 1e-05
BF = jnp.bfloat16
F32 = jnp.float32
FACTOR = HEAD ** (-0.5)
SHARE = 20


def dot(a, b, ca, cb):
    return lax.dot_general(a, b, (((ca,), (cb,)), ((), ())), preferred_element_type=F32)


def pair_of(xh, co):
    return co * 2 + xh


def window_of(pair):
    return (pair // 2) * 384 + (pair % 2) * 128


def head_lanes(pair, head, rows):
    lane = lax.broadcasted_iota(jnp.int32, (rows, 256), 1) - ((pair % 2) * 64 + head * HEAD)
    return (lane >= 0) & (lane < HEAD)


def by_head(x, pair):
    zero = jnp.zeros_like(x)
    return jnp.concatenate([jnp.where(head_lanes(pair, h, x.shape[0]), x, zero) for h in range(2)], axis=0)


def layer_stats(x):
    centred = x - jnp.mean(x, axis=-1, keepdims=True)
    inverse = lax.rsqrt(jnp.mean(centred * centred, axis=-1, keepdims=True) + EPS)
    return centred * inverse, inverse


def slot_image(owner_ref, section, slot):
    found = jnp.int32(0)
    index = jnp.int32(0)
    seen = jnp.int32(0)
    for i in range(IMGS):
        mine = (owner_ref[0, i] == section).astype(jnp.int32)
        take = (mine == 1) & (seen == slot)
        index = jnp.where(take, i, index)
        found = jnp.where(take, 1, found)
        seen = seen + mine
    return index, found


def scale_of(sample_ref, i):
    count = jnp.int32(0)
    for k in range(IMGS):
        count = count + (sample_ref[0, k] == sample_ref[0, i]).astype(jnp.int32)
    return count


AROUND = ((0, 0), (0, 1), (1, 0), (1, 1))


def attn_kernel(owner_ref, part_ref, c1_ref, ow_ref, lat_ref, mine, far, u_ref, chip, prod):
    xh = lax.axis_index("xh")
    co = lax.axis_index("co")
    chip[...] = (part_ref[...].astype(F32) + c1_ref[...].astype(F32)).astype(BF)
    group = ow_ref[pl.ds(pl.multiple_of(co * 384, 128), 384)]
    prod[...] = dot(chip[...].reshape(IMGS * LAT, D), group, 1, 1).astype(BF)
    mine[...] = prod[:, pl.ds(pl.multiple_of(xh * 128, 128), 256)]
    far[...] = prod[:, pl.ds(pl.multiple_of((1 - xh) * 128, 128), 256)]
    for slot in range(2):
        index, _ = slot_image(owner_ref, (xh ^ 1) * 2 + co, slot)
        u_ref[slot] = chip[index]


def forward_kernel(feat_ref, lat_ref, fg_ref, lg_ref, qw_hbm, kvw_hbm, ctx_ref, kv_ref, q_ref, pr_ref, win, sems):
    pair = pair_of(lax.axis_index("xh"), lax.axis_index("co"))
    start = pl.multiple_of(window_of(pair), 128)
    copies = [
        pltpu.make_async_copy(qw_hbm.at[:, pl.ds(start, 256)], win.at[0], sems.at[0]),
        pltpu.make_async_copy(kvw_hbm.at[:, pl.ds(start, 256)], win.at[1], sems.at[1]),
        pltpu.make_async_copy(kvw_hbm.at[:, pl.ds(pl.multiple_of(start + INNER, 128), 256)], win.at[2], sems.at[2]),
    ]
    for c in copies:
        c.start()
    fg = fg_ref[...].reshape(1, D)
    lg = lg_ref[...].reshape(1, D)
    live = lax.broadcasted_iota(jnp.int32, (2 * LAT, ROWS), 1) < TOK

    def norm(i):
        for c in range(4):
            hat, _ = layer_stats(feat_ref[i, 64 * c:64 * (c + 1)].astype(F32))
            ctx_ref[i, LAT + 64 * c:LAT + 64 * (c + 1)] = (hat * fg).astype(BF)
        hat, _ = layer_stats(lat_ref[i].astype(F32))
        ctx_ref[i, :LAT] = (hat * lg).astype(BF)
        hat, _ = layer_stats(feat_ref[i, 256:257].astype(F32))
        first = lax.broadcasted_iota(jnp.int32, (16, D), 0) == 0
        ctx_ref[i, 320:ROWS] = jnp.where(first, hat * fg, 0.0).astype(BF)

    def project(i):
        kv_ref[i, :, :256] = dot(ctx_ref[i], win[1], 1, 0).astype(BF)
        kv_ref[i, :, 256:] = dot(ctx_ref[i], win[2], 1, 0).astype(BF)
        q_ref[i] = by_head(dot(ctx_ref[i, :LAT], win[0], 1, 0), pair).astype(BF)

    def attend(i):
        scores = dot(q_ref[i], kv_ref[i, :, :256], 1, 1) * FACTOR
        scores = jnp.where(live, scores, -1e30)
        shifted = jnp.exp(scores - jnp.max(scores, axis=-1, keepdims=True))
        shifted = jnp.where(live, shifted, 0.0)
        pr_ref[i] = shifted / jnp.sum(shifted, axis=-1, keepdims=True)

    norm(0)
    for c in copies:
        c.wait()
    for i in range(IMGS):
        if i < IMGS - 1:
            norm(i + 1)
        project(i)
        if i > 0:
            attend(i - 1)
    attend(IMGS - 1)


def backward_kernel(owner_ref, sample_ref, a0, a2, kv_ref, q_ref, pr_ref,
                    kvg, g0, g1, g2, lat):
    xh = lax.axis_index("xh")
    co = lax.axis_index("co")
    pair = pair_of(xh, co)
    left = lax.broadcasted_iota(jnp.int32, (ROWS, 128), 1) < 64
    for i in range(IMGS):
        rows = slice(LAT * i, LAT * (i + 1))
        count = scale_of(sample_ref, i).astype(F32)
        total = a0[rows].astype(F32) + a2[rows].astype(F32)
        attn = by_head(total / count, pair).astype(BF)
        probs = pr_ref[i]
        value_grad = dot(probs.astype(BF), attn, 0, 0)
        prob_grad = dot(attn, kv_ref[i, :, 256:], 1, 1)
        inner = jnp.sum(probs * prob_grad, axis=-1, keepdims=True)
        score_grad = (probs * (prob_grad - inner) * FACTOR).astype(BF)
        query_grad = dot(score_grad, kv_ref[i, :, :256], 1, 0)
        query_grad = jnp.where(head_lanes(pair, 0, LAT), query_grad[:LAT],
                               jnp.where(head_lanes(pair, 1, LAT), query_grad[LAT:], 0.0))
        key_grad = dot(score_grad, q_ref[i], 0, 0)
        lat[rows, :256] = query_grad.astype(BF)
        lat[rows, 256:512] = key_grad[:LAT].astype(BF)
        lat[rows, 512:] = value_grad[:LAT].astype(BF)
        at = slice(ROWS * i, ROWS * (i + 1))
        kvg[at, :128] = jnp.where(xh == 0, key_grad[:, :128], key_grad[:, 128:]).astype(BF)
        kvg[at, 128:256] = jnp.where(xh == 0, value_grad[:, :128], value_grad[:, 128:]).astype(BF)
        even = jnp.where(left, key_grad[:, 128:], pltpu.roll(value_grad[:, 128:], 64, 1))
        odd = jnp.where(left, pltpu.roll(key_grad[:, :128], 64, 1), value_grad[:, :128])
        kvg[at, 256:] = jnp.where(xh == 0, even, odd).astype(BF)
    places = (g0, g1.at[:2 * LAT], g2, g1.at[2 * LAT:])
    for out, (dx, dc) in zip(places, AROUND):
        section = (xh ^ dx) * 2 + (co ^ dc)
        for slot in range(2):
            index, _ = slot_image(owner_ref, section, slot)
            out[LAT * slot:LAT * (slot + 1)] = lat[pl.ds(pl.multiple_of(index * LAT, LAT), LAT)]


def weight_kernel(ctx_ref, kvg, w_ref, wide, order):
    ctx = ctx_ref[...].reshape(IMGS * ROWS, D)
    for c in range(5):
        wide[256 * c:256 * (c + 1)] = dot(ctx[:, 256 * c:256 * (c + 1)], kvg[...], 0, 0)
    for y in range(4):
        for xl in range(2):
            piece = xl * 4 + y
            for z in range(8):
                first = ((z * 4 + y) * 2 + xl) * SHARE
                order[piece, z * SHARE:(z + 1) * SHARE] = wide[first:first + SHARE]
            whole = order[piece]
            keys = whole[:, :128], whole[:, 256:320]
            vals = whole[:, 128:256], whole[:, 320:]
            for k, (main, tail) in enumerate((keys, vals)):
                w_ref[8 * k + piece, 0:160] = main.astype(BF)
                w_ref[8 * k + piece, 160:240] = jnp.concatenate([tail[:80], tail[80:]], axis=1).astype(BF)


def first_sum_kernel(r_ref, out_ref, full):
    tails = []
    for k in range(2):
        total = r_ref[8 * k].astype(F32)
        for p in range(1, 8):
            total = total + r_ref[8 * k + p].astype(F32)
        full[:, 256 * k:256 * k + 128] = total[:160]
        tail = total[160:]
        tails.append(jnp.concatenate([tail[:, :64], tail[:, 64:]], axis=0))
    full[:, 128:256] = jnp.concatenate(tails, axis=1)
    for z in range(8):
        out_ref[z, 0:SHARE] = full[SHARE * z:SHARE * (z + 1)].astype(BF)


def last_kernel(r_ref, out_ref):
    total = r_ref[0].astype(F32)
    for z in range(1, 8):
        total = total + r_ref[z].astype(F32)
    out_ref[...] = total[:SHARE] * (1.0 / 256.0)


def latent_kernel(owner_ref, sample_ref, part_ref, lat_ref, lg_ref, qw_hbm, kvw_hbm,
                  c1, u2, g0, g1, g2, out_ref, win, sems):
    xh = lax.axis_index("xh")
    co = lax.axis_index("co")
    section = xh * 2 + co
    copies = []
    for dx, dc in AROUND:
        start = pl.multiple_of(window_of(pair_of(xh ^ dx, co ^ dc)), 128)
        further = pl.multiple_of(start + INNER, 128)
        for k, (source, lane) in enumerate(((qw_hbm, start), (kvw_hbm, start), (kvw_hbm, further))):
            n = len(copies)
            copies.append(pltpu.make_async_copy(source.at[:, pl.ds(lane, 256)], win.at[n], sems.at[n]))
    for c in copies:
        c.start()
    sources = (g0, g1.at[:2 * LAT], g2.at[:2 * LAT], g2.at[2 * LAT:])
    grad = jnp.zeros((2 * LAT, D), F32)
    for n, c in enumerate(copies):
        c.wait()
        k = n % 3
        grad = grad + dot(sources[n // 3][:, 256 * k:256 * (k + 1)], win[n], 1, 1)
    lg = lg_ref[...].reshape(1, D)
    for slot in range(2):
        index, found = slot_image(owner_ref, section, slot)
        count = scale_of(sample_ref, index).astype(F32)
        summed = (part_ref[index].astype(F32) + c1[index].astype(F32)) + u2[slot].astype(F32)
        upstream = (summed / count).astype(BF).astype(F32)
        hat, inverse = layer_stats(lat_ref[index].astype(F32))
        dy = grad[LAT * slot:LAT * (slot + 1)] * lg
        centred = dy - jnp.mean(dy, axis=-1, keepdims=True) - hat * jnp.mean(dy * hat, axis=-1, keepdims=True)
        out = (upstream + inverse * centred).astype(BF)
        out_ref[slot] = jnp.where(found == 1, out, jnp.zeros_like(out))


SMEM = pl.BlockSpec(memory_space=pltpu.SMEM)
VMEM = pl.BlockSpec(memory_space=pltpu.VMEM)
HBM = pl.BlockSpec(memory_space=pltpu.HBM)
CORE = [(0, 1), (1, 0), (2, 3), (3, 2)]
FAR = [(0, 2), (2, 0), (1, 3), (3, 1)]
DIAGONAL = [(0, 3), (3, 0), (1, 2), (2, 1)]
SECTION = ("xh", "co")


def call(body, name, outs, ins, scratch=(), flops=0, size=0, limit=24):
    return pl.pallas_call(
        body,
        out_shape=outs,
        in_specs=ins,
        out_specs=jax.tree.map(lambda _: VMEM, outs),
        scratch_shapes=list(scratch),
        cost_estimate=pl.CostEstimate(flops=flops, bytes_accessed=size, transcendentals=0),
        compiler_params=pltpu.CompilerParams(vmem_limit_bytes=limit * 2**20),
        name=name,
    )


def swap(x, pairs):
    return lax.ppermute(x, SECTION, pairs)


def bf(*shape):
    return jax.ShapeDtypeStruct(shape, BF)


DMA = pltpu.SemaphoreType.DMA
COST = 1000000
CALLS = dict(
    attn=call(
        attn_kernel, "attn_part", [bf(256, 256)] * 2 + [bf(2, LAT, D)], [SMEM] + [VMEM] * 4,
        [pltpu.VMEM((IMGS, LAT, D), BF), pltpu.VMEM((256, 384), BF)],
        flops=600_000_000, size=3_000_000),
    forward=call(
        forward_kernel, "forward_part",
        [bf(IMGS, ROWS, D), bf(IMGS, ROWS, 512), bf(IMGS, 2 * LAT, 256),
         jax.ShapeDtypeStruct((IMGS, 2 * LAT, ROWS), F32)],
        [VMEM] * 4 + [HBM] * 2,
        [pltpu.VMEM((3, D, 256), BF), DMA((3,))],
        flops=4_000_000_000, size=12_000_000),
    backward=call(
        backward_kernel, "backward_part", [bf(IMGS * ROWS, 384)] + [bf(2 * LAT, 768), bf(4 * LAT, 768), bf(2 * LAT, 768)],
        [SMEM, SMEM] + [VMEM] * 5, [pltpu.VMEM((256, 768), BF)],
        flops=COST, size=1000),
    weight=call(
        weight_kernel, "weight_part", bf(16, 240, 128), [VMEM] * 2,
        [pltpu.VMEM((D, 384), F32), pltpu.VMEM((8, 160, 384), F32)],
        flops=COST, size=1000),
    first=call(first_sum_kernel, "first_sum", bf(8, 32, 384), [VMEM], [pltpu.VMEM((160, 384), F32)],
               size=1_000_000),
    last=call(last_kernel, "last_sum", jax.ShapeDtypeStruct((SHARE, 384), F32), [VMEM], size=300_000),
    latent=call(
        latent_kernel, "latent_part", bf(2, LAT, D), [SMEM, SMEM] + [VMEM] * 3 + [HBM] * 2 + [VMEM] * 5,
        [pltpu.VMEM((12, D, 256), BF), DMA((12,))],
        flops=2_000_000_000, size=9_000_000, limit=52),
)


def per_device(partials, latents, features, feature_gain, latent_gain, query_weight, kv_weight, out_weight,
               sample_of, owner):
    part = partials[0]
    owner = owner.reshape(1, IMGS)
    c1 = swap(part, CORE)
    a0, a2, u = CALLS["attn"](owner, part, c1, out_weight, latents)
    a2 = swap(a2, FAR)
    u = swap(u, FAR)
    ctx, kv, q, probs = CALLS["forward"](
        features, latents, feature_gain, latent_gain, query_weight, kv_weight)
    kvg, g0, g1, g2 = CALLS["backward"](owner, sample_of, a0, a2, kv, q, probs)
    g1 = swap(g1, CORE)
    g2 = jnp.concatenate([g2, g1[2 * LAT:]], axis=0)
    w = CALLS["weight"](ctx, kvg)
    w, u = lax.optimization_barrier((w, u))
    w = lax.all_to_all(w, ("xh", "xl", "y"), 0, 0, tiled=True)
    w, g2 = lax.optimization_barrier((w, g2))
    g2 = swap(g2, FAR)
    w = CALLS["first"](w)
    latent_grad = CALLS["latent"](
        owner, sample_of, part, latents, latent_gain, query_weight, kv_weight, c1, u, g0, g1, g2)
    w = lax.all_to_all(w, "z", 0, 0, tiled=True)
    w, latent_grad = lax.optimization_barrier((w, latent_grad))
    kv_grad = CALLS["last"](w)
    return latent_grad[None], kv_grad


def solution(mesh):
    fine = Mesh(mesh.devices.reshape(2, 2, 8, 4, 2), ("xh", "co", "z", "y", "xl"))
    dp = ("z", "y", "xl")
    return jax.shard_map(
        per_device,
        mesh=fine,
        in_specs=(
            P(SECTION, dp, None, None),
            P(dp, None, None),
            P(dp, None, None),
            P(),
            P(),
            P(),
            P(),
            P(),
            P(dp, None),
            P(dp, None),
        ),
        out_specs=(P(SECTION, dp, None, None), P(dp, SECTION)),
        check_vma=False,
    )
```

```python
import functools
import jax
import jax.numpy as jnp
from jax import lax
from jax.experimental import pallas as pl
from jax.experimental.pallas import tpu as pltpu
from jax.sharding import Mesh, PartitionSpec as P

HEAD = 96
IMGS = 4
LAT = 64
PATCH = 257
TOK = 321
ROWS = 336
D = 1280
INNER = 768
EPS = 1e-05
BF = jnp.bfloat16
F32 = jnp.float32
FACTOR = HEAD ** (-0.5)
SHARE = 20


def dot(a, b, ca, cb):
    return lax.dot_general(a, b, (((ca,), (cb,)), ((), ())), preferred_element_type=F32)


def pair_of(xh, co):
    return co * 2 + xh


def window_of(pair):
    return (pair // 2) * 384 + (pair % 2) * 128


def head_lanes(pair, head, rows):
    lane = lax.broadcasted_iota(jnp.int32, (rows, 256), 1) - ((pair % 2) * 64 + head * HEAD)
    return (lane >= 0) & (lane < HEAD)


def by_head(x, pair):
    zero = jnp.zeros_like(x)
    return jnp.concatenate([jnp.where(head_lanes(pair, h, x.shape[0]), x, zero) for h in range(2)], axis=0)


def layer_stats(x):
    centred = x - jnp.mean(x, axis=-1, keepdims=True)
    inverse = lax.rsqrt(jnp.mean(centred * centred, axis=-1, keepdims=True) + EPS)
    return centred * inverse, inverse


def slot_image(owner_ref, section, slot):
    found = jnp.int32(0)
    index = jnp.int32(0)
    seen = jnp.int32(0)
    for i in range(IMGS):
        mine = (owner_ref[0, i] == section).astype(jnp.int32)
        take = (mine == 1) & (seen == slot)
        index = jnp.where(take, i, index)
        found = jnp.where(take, 1, found)
        seen = seen + mine
    return index, found


def scale_of(sample_ref, i):
    count = jnp.int32(0)
    for k in range(IMGS):
        count = count + (sample_ref[0, k] == sample_ref[0, i]).astype(jnp.int32)
    return count


AROUND = ((0, 0), (0, 1), (1, 0), (1, 1))


def attn_kernel(owner_ref, part_ref, c1_ref, ow_ref, lat_ref, mine, far, u_ref, chip, prod):
    xh = lax.axis_index("xh")
    co = lax.axis_index("co")
    chip[...] = (part_ref[...].astype(F32) + c1_ref[...].astype(F32)).astype(BF)
    group = ow_ref[pl.ds(pl.multiple_of(co * 384, 128), 384)]
    prod[...] = dot(chip[...].reshape(IMGS * LAT, D), group, 1, 1)
    mine[...] = prod[:, pl.ds(pl.multiple_of(xh * 128, 128), 256)]
    far[...] = prod[:, pl.ds(pl.multiple_of((1 - xh) * 128, 128), 256)].astype(BF)
    for slot in range(2):
        index, _ = slot_image(owner_ref, (xh ^ 1) * 2 + co, slot)
        u_ref[slot] = chip[index]


def forward_kernel(feat_ref, lat_ref, fg_ref, lg_ref, qw_hbm, kvw_hbm, ctx_ref, kv_ref, q_ref, pr_ref, win, sems):
    pair = pair_of(lax.axis_index("xh"), lax.axis_index("co"))
    start = pl.multiple_of(window_of(pair), 128)
    copies = [
        pltpu.make_async_copy(qw_hbm.at[:, pl.ds(start, 256)], win.at[0], sems.at[0]),
        pltpu.make_async_copy(kvw_hbm.at[:, pl.ds(start, 256)], win.at[1], sems.at[1]),
        pltpu.make_async_copy(kvw_hbm.at[:, pl.ds(pl.multiple_of(start + INNER, 128), 256)], win.at[2], sems.at[2]),
    ]
    for c in copies:
        c.start()
    fg = fg_ref[...].reshape(1, D)
    lg = lg_ref[...].reshape(1, D)
    live = lax.broadcasted_iota(jnp.int32, (2 * LAT, ROWS), 1) < TOK

    def norm(i):
        for c in range(4):
            hat, _ = layer_stats(feat_ref[i, 64 * c:64 * (c + 1)].astype(F32))
            ctx_ref[i, LAT + 64 * c:LAT + 64 * (c + 1)] = (hat * fg).astype(BF)
        hat, _ = layer_stats(lat_ref[i].astype(F32))
        ctx_ref[i, :LAT] = (hat * lg).astype(BF)
        hat, _ = layer_stats(feat_ref[i, 256:257].astype(F32))
        first = lax.broadcasted_iota(jnp.int32, (16, D), 0) == 0
        ctx_ref[i, 320:ROWS] = jnp.where(first, hat * fg, 0.0).astype(BF)

    def project(i):
        kv_ref[i, :, :256] = dot(ctx_ref[i], win[1], 1, 0).astype(BF)
        kv_ref[i, :, 256:] = dot(ctx_ref[i], win[2], 1, 0).astype(BF)
        q_ref[i] = by_head(dot(ctx_ref[i, :LAT], win[0], 1, 0), pair).astype(BF)

    def attend(i):
        scores = dot(q_ref[i], kv_ref[i, :, :256], 1, 1) * FACTOR
        scores = jnp.where(live, scores, -1e30)
        shifted = jnp.exp(scores - jnp.max(scores, axis=-1, keepdims=True))
        shifted = jnp.where(live, shifted, 0.0)
        pr_ref[i] = shifted / jnp.sum(shifted, axis=-1, keepdims=True)

    norm(0)
    for c in copies:
        c.wait()
    for i in range(IMGS):
        if i < IMGS - 1:
            norm(i + 1)
        project(i)
        if i > 0:
            attend(i - 1)
    attend(IMGS - 1)


def backward_kernel(owner_ref, sample_ref, a0, a2, kv_ref, q_ref, pr_ref,
                    kvg, g0, g1, g2, lat):
    xh = lax.axis_index("xh")
    co = lax.axis_index("co")
    pair = pair_of(xh, co)
    left = lax.broadcasted_iota(jnp.int32, (ROWS, 128), 1) < 64
    for i in range(IMGS):
        rows = slice(LAT * i, LAT * (i + 1))
        count = scale_of(sample_ref, i).astype(F32)
        total = a0[rows] + a2[rows].astype(F32)
        attn = by_head(total / count, pair).astype(BF)
        probs = pr_ref[i]
        value_grad = dot(probs.astype(BF), attn, 0, 0)
        prob_grad = dot(attn, kv_ref[i, :, 256:], 1, 1)
        inner = jnp.sum(probs * prob_grad, axis=-1, keepdims=True)
        score_grad = (probs * (prob_grad - inner) * FACTOR).astype(BF)
        query_grad = dot(score_grad, kv_ref[i, :, :256], 1, 0)
        query_grad = jnp.where(head_lanes(pair, 0, LAT), query_grad[:LAT],
                               jnp.where(head_lanes(pair, 1, LAT), query_grad[LAT:], 0.0))
        key_grad = dot(score_grad, q_ref[i], 0, 0)
        lat[rows, :256] = query_grad.astype(BF)
        lat[rows, 256:512] = key_grad[:LAT].astype(BF)
        lat[rows, 512:] = value_grad[:LAT].astype(BF)
        at = slice(ROWS * i, ROWS * (i + 1))
        kvg[at, :128] = jnp.where(xh == 0, key_grad[:, :128], key_grad[:, 128:]).astype(BF)
        kvg[at, 128:256] = jnp.where(xh == 0, value_grad[:, :128], value_grad[:, 128:]).astype(BF)
        even = jnp.where(left, key_grad[:, 128:], pltpu.roll(value_grad[:, 128:], 64, 1))
        odd = jnp.where(left, pltpu.roll(key_grad[:, :128], 64, 1), value_grad[:, :128])
        kvg[at, 256:] = jnp.where(xh == 0, even, odd).astype(BF)
    places = (g0, g1.at[:2 * LAT], g2, g1.at[2 * LAT:])
    for out, (dx, dc) in zip(places, AROUND):
        section = (xh ^ dx) * 2 + (co ^ dc)
        for slot in range(2):
            index, _ = slot_image(owner_ref, section, slot)
            out[LAT * slot:LAT * (slot + 1)] = lat[pl.ds(pl.multiple_of(index * LAT, LAT), LAT)]


def weight_kernel(ctx_ref, kvg, w_ref, wide, order):
    ctx = ctx_ref[...].reshape(IMGS * ROWS, D)
    for c in range(5):
        columns = slice(256 * c, 256 * (c + 1))
        wide[columns] = dot(ctx[:, columns], kvg[...], 0, 0)
    for y in range(4):
        for xl in range(2):
            piece = xl * 4 + y
            for z in range(8):
                first = ((z * 4 + y) * 2 + xl) * SHARE
                order[piece, z * SHARE:(z + 1) * SHARE] = wide[first:first + SHARE]
            whole = order[piece]
            keys = whole[:, :128], whole[:, 256:320]
            vals = whole[:, 128:256], whole[:, 320:]
            for k, (main, tail) in enumerate((keys, vals)):
                w_ref[8 * k + piece, 0:160] = main.astype(BF)
                w_ref[8 * k + piece, 160:240] = jnp.concatenate([tail[:80], tail[80:]], axis=1).astype(BF)


def first_sum_kernel(r_ref, out_ref, full, share):
    tails = []
    for k in range(2):
        total = r_ref[8 * k].astype(F32)
        for p in range(1, 8):
            total = total + r_ref[8 * k + p].astype(F32)
        full[:, 256 * k:256 * k + 128] = total[:160]
        tail = total[160:]
        tails.append(jnp.concatenate([tail[:, :64], tail[:, 64:]], axis=0))
    full[:, 128:256] = jnp.concatenate(tails, axis=1)
    for z in range(8):
        for k in range(3):
            share[z, SHARE * k:SHARE * (k + 1)] = full[SHARE * z:SHARE * (z + 1), 128 * k:128 * (k + 1)]
        share[z, 3 * SHARE:] = jnp.zeros((64 - 3 * SHARE, 128), F32)
    out_ref[...] = share[...].astype(BF)


def last_kernel(r_ref, out_ref):
    total = r_ref[0].astype(F32)
    for z in range(1, 8):
        total = total + r_ref[z].astype(F32)
    total = total * (1.0 / 256.0)
    for k in range(3):
        out_ref[:, 128 * k:128 * (k + 1)] = total[SHARE * k:SHARE * (k + 1)]


def latent_kernel(owner_ref, sample_ref, part_ref, lat_ref, lg_ref, qw_hbm, kvw_hbm,
                  c1, u2, g0, g1, g2, out_ref, qw, kvw, every, grad, sems):
    xh = lax.axis_index("xh")
    co = lax.axis_index("co")
    section = xh * 2 + co
    copies = []
    for c in range(5):
        rows = pl.ds(256 * c, 256)
        copies.append((pltpu.make_async_copy(qw_hbm.at[rows], qw.at[rows], sems.at[2 * c]),
                       pltpu.make_async_copy(kvw_hbm.at[rows], kvw.at[rows], sems.at[2 * c + 1])))
    for pair in copies:
        for c in pair:
            c.start()
    near = (co, g0[...], g2[:2 * LAT])
    other = (1 - co, g1[:2 * LAT], g2[2 * LAT:])
    for group, same, across in (near, other):
        even = jnp.where(xh == 0, same, across)
        odd = jnp.where(xh == 0, across, same)
        for k in range(3):
            first = pl.multiple_of(group * 384 + INNER * k, 128)
            e = even[:, 256 * k:256 * (k + 1)]
            o = odd[:, 256 * k:256 * (k + 1)]
            every[:, pl.ds(first, 128)] = e[:, :128]
            every[:, pl.ds(pl.multiple_of(first + 128, 128), 128)] = e[:, 128:] + o[:, :128]
            every[:, pl.ds(pl.multiple_of(first + 256, 128), 128)] = o[:, 128:]
    for c, pair in enumerate(copies):
        for one in pair:
            one.wait()
        rows = slice(256 * c, 256 * (c + 1))
        block = dot(qw[rows], every[:, :INNER], 1, 1) + dot(kvw[rows], every[:, INNER:], 1, 1)
        grad[:, rows] = jnp.transpose(block)
    lg = lg_ref[...].reshape(1, D)
    for slot in range(2):
        index, found = slot_image(owner_ref, section, slot)
        count = scale_of(sample_ref, index).astype(F32)
        summed = (part_ref[index].astype(F32) + c1[index].astype(F32)) + u2[slot].astype(F32)
        upstream = (summed / count).astype(BF).astype(F32)
        hat, inverse = layer_stats(lat_ref[index].astype(F32))
        dy = grad[LAT * slot:LAT * (slot + 1)] * lg
        centred = dy - jnp.mean(dy, axis=-1, keepdims=True) - hat * jnp.mean(dy * hat, axis=-1, keepdims=True)
        out = (upstream + inverse * centred).astype(BF)
        out_ref[slot] = jnp.where(found == 1, out, jnp.zeros_like(out))


SMEM = pl.BlockSpec(memory_space=pltpu.SMEM)
VMEM = pl.BlockSpec(memory_space=pltpu.VMEM)
HBM = pl.BlockSpec(memory_space=pltpu.HBM)
CORE = [(0, 1), (1, 0), (2, 3), (3, 2)]
FAR = [(0, 2), (2, 0), (1, 3), (3, 1)]
DIAGONAL = [(0, 3), (3, 0), (1, 2), (2, 1)]
SECTION = ("xh", "co")


def call(body, name, outs, ins, scratch=(), flops=0, size=0, limit=24):
    return pl.pallas_call(
        body,
        out_shape=outs,
        in_specs=ins,
        out_specs=jax.tree.map(lambda _: VMEM, outs),
        scratch_shapes=list(scratch),
        cost_estimate=pl.CostEstimate(flops=flops, bytes_accessed=size, transcendentals=0),
        compiler_params=pltpu.CompilerParams(vmem_limit_bytes=limit * 2**20),
        name=name,
    )


def swap(x, pairs):
    return lax.ppermute(x, SECTION, pairs)


def bf(*shape):
    return jax.ShapeDtypeStruct(shape, BF)


DMA = pltpu.SemaphoreType.DMA
COST = 1000000
CALLS = dict(
    attn=call(
        attn_kernel, "attn_part", [jax.ShapeDtypeStruct((256, 256), F32), bf(256, 256), bf(2, LAT, D)], [SMEM] + [VMEM] * 4,
        [pltpu.VMEM((IMGS, LAT, D), BF), pltpu.VMEM((256, 384), F32)],
        flops=600_000_000, size=3_000_000),
    forward=call(
        forward_kernel, "forward_part",
        [bf(IMGS, ROWS, D), bf(IMGS, ROWS, 512), bf(IMGS, 2 * LAT, 256),
         jax.ShapeDtypeStruct((IMGS, 2 * LAT, ROWS), F32)],
        [VMEM] * 4 + [HBM] * 2,
        [pltpu.VMEM((3, D, 256), BF), DMA((3,))],
        flops=4_000_000_000, size=12_000_000),
    backward=call(
        backward_kernel, "backward_part",
        [bf(IMGS * ROWS, 384), bf(2 * LAT, 768), bf(4 * LAT, 768), bf(2 * LAT, 768)],
        [SMEM, SMEM] + [VMEM] * 5, [pltpu.VMEM((256, 768), BF)],
        flops=COST, size=1000),
    weight=call(
        weight_kernel, "weight_part", bf(16, 240, 128), [VMEM] * 2,
        [pltpu.VMEM((D, 384), F32), pltpu.VMEM((8, 160, 384), F32)],
        flops=COST, size=1000),
    first=call(first_sum_kernel, "first_sum", bf(8, 64, 128), [VMEM],
               [pltpu.VMEM((160, 384), F32), pltpu.VMEM((8, 64, 128), F32)],
               size=1_000_000),
    last=call(last_kernel, "last_sum", jax.ShapeDtypeStruct((SHARE, 384), F32), [VMEM], size=300_000),
    latent=call(
        latent_kernel, "latent_part", bf(2, LAT, D), [SMEM, SMEM] + [VMEM] * 3 + [HBM] * 2 + [VMEM] * 5,
        [pltpu.VMEM((D, INNER), BF), pltpu.VMEM((D, 2 * INNER), BF), pltpu.VMEM((2 * LAT, 3 * INNER), BF),
         pltpu.VMEM((2 * LAT, D), F32), DMA((10,))],
        flops=2_000_000_000, size=9_000_000, limit=52),
)


def per_device(partials, latents, features, feature_gain, latent_gain, query_weight, kv_weight, out_weight,
               sample_of, owner):
    part = partials[0]
    owner = owner.reshape(1, IMGS)
    c1 = swap(part, CORE)
    a0, a2, u = CALLS["attn"](owner, part, c1, out_weight, latents)
    a2 = swap(a2, FAR)
    u = swap(u, FAR)
    ctx, kv, q, probs = CALLS["forward"](
        features, latents, feature_gain, latent_gain, query_weight, kv_weight)
    kvg, g0, g1, g2 = CALLS["backward"](owner, sample_of, a0, a2, kv, q, probs)
    g1 = swap(g1, CORE)
    g2 = jnp.concatenate([g2, g1[2 * LAT:]], axis=0)
    w = CALLS["weight"](ctx, kvg)
    w, u = lax.optimization_barrier((w, u))
    w = lax.all_to_all(w, ("xh", "xl", "y"), 0, 0, tiled=True)
    w, g2 = lax.optimization_barrier((w, g2))
    g2 = swap(g2, FAR)
    w = CALLS["first"](w)
    latent_grad = CALLS["latent"](
        owner, sample_of, part, latents, latent_gain, query_weight, kv_weight, c1, u, g0, g1, g2)
    w = lax.all_to_all(w, "z", 0, 0, tiled=True)
    w, latent_grad = lax.optimization_barrier((w, latent_grad))
    kv_grad = CALLS["last"](w)
    return latent_grad[None], kv_grad


def solution(mesh):
    fine = Mesh(mesh.devices.reshape(2, 2, 8, 4, 2), ("xh", "co", "z", "y", "xl"))
    dp = ("z", "y", "xl")
    return jax.shard_map(
        per_device,
        mesh=fine,
        in_specs=(
            P(SECTION, dp, None, None),
            P(dp, None, None),
            P(dp, None, None),
            P(),
            P(),
            P(),
            P(),
            P(),
            P(dp, None),
            P(dp, None),
        ),
        out_specs=(P(SECTION, dp, None, None), P(dp, SECTION)),
        check_vma=False,
    )
```

```python
import functools
import jax
import jax.numpy as jnp
from jax import lax
from jax.experimental import pallas as pl
from jax.experimental.pallas import tpu as pltpu
from jax.sharding import Mesh, PartitionSpec as P

HEAD = 96
IMGS = 4
LAT = 64
PATCH = 257
TOK = 321
ROWS = 336
D = 1280
INNER = 768
EPS = 1e-05
BF = jnp.bfloat16
F32 = jnp.float32
FACTOR = HEAD ** (-0.5)
SHARE = 20


def dot(a, b, ca, cb):
    return lax.dot_general(a, b, (((ca,), (cb,)), ((), ())), preferred_element_type=F32)


def pair_of(xh, co):
    return co * 2 + xh


def window_of(pair):
    return (pair // 2) * 384 + (pair % 2) * 128


def head_lanes(pair, head, rows):
    lane = lax.broadcasted_iota(jnp.int32, (rows, 256), 1) - ((pair % 2) * 64 + head * HEAD)
    return (lane >= 0) & (lane < HEAD)


def by_head(x, pair):
    zero = jnp.zeros_like(x)
    return jnp.concatenate([jnp.where(head_lanes(pair, h, x.shape[0]), x, zero) for h in range(2)], axis=0)


def layer_stats(x):
    centred = x - jnp.mean(x, axis=-1, keepdims=True)
    inverse = lax.rsqrt(jnp.mean(centred * centred, axis=-1, keepdims=True) + EPS)
    return centred * inverse, inverse


def slot_image(owner_ref, section, slot):
    found = jnp.int32(0)
    index = jnp.int32(0)
    seen = jnp.int32(0)
    for i in range(IMGS):
        mine = (owner_ref[0, i] == section).astype(jnp.int32)
        take = (mine == 1) & (seen == slot)
        index = jnp.where(take, i, index)
        found = jnp.where(take, 1, found)
        seen = seen + mine
    return index, found


def scale_of(sample_ref, i):
    count = jnp.int32(0)
    for k in range(IMGS):
        count = count + (sample_ref[0, k] == sample_ref[0, i]).astype(jnp.int32)
    return count


AROUND = ((0, 0), (0, 1), (1, 0), (1, 1))


def attn_kernel(owner_ref, part_ref, c1_ref, ow_ref, lat_ref, mine, far, u_ref, chip, prod):
    xh = lax.axis_index("xh")
    co = lax.axis_index("co")
    chip[...] = (part_ref[...].astype(F32) + c1_ref[...].astype(F32)).astype(BF)
    group = ow_ref[pl.ds(pl.multiple_of(co * 384, 128), 384)]
    prod[...] = dot(chip[...].reshape(IMGS * LAT, D), group, 1, 1)
    mine[...] = prod[:, pl.ds(pl.multiple_of(xh * 128, 128), 256)]
    far[...] = prod[:, pl.ds(pl.multiple_of((1 - xh) * 128, 128), 256)].astype(BF)
    for slot in range(2):
        index, _ = slot_image(owner_ref, (xh ^ 1) * 2 + co, slot)
        u_ref[slot] = chip[index]


def forward_kernel(feat_ref, lat_ref, fg_ref, lg_ref, qw_hbm, kvw_hbm, ctx_ref, kv_ref, q_ref, pr_ref, win, sems):
    pair = pair_of(lax.axis_index("xh"), lax.axis_index("co"))
    start = pl.multiple_of(window_of(pair), 128)
    copies = [
        pltpu.make_async_copy(qw_hbm.at[:, pl.ds(start, 256)], win.at[0], sems.at[0]),
        pltpu.make_async_copy(kvw_hbm.at[:, pl.ds(start, 256)], win.at[1], sems.at[1]),
        pltpu.make_async_copy(kvw_hbm.at[:, pl.ds(pl.multiple_of(start + INNER, 128), 256)], win.at[2], sems.at[2]),
    ]
    for c in copies:
        c.start()
    fg = fg_ref[...].reshape(1, D)
    lg = lg_ref[...].reshape(1, D)
    live = lax.broadcasted_iota(jnp.int32, (2 * LAT, ROWS), 1) < TOK

    def norm(i):
        for c in range(4):
            hat, _ = layer_stats(feat_ref[i, 64 * c:64 * (c + 1)].astype(F32))
            ctx_ref[i, LAT + 64 * c:LAT + 64 * (c + 1)] = (hat * fg).astype(BF)
        hat, _ = layer_stats(lat_ref[i].astype(F32))
        ctx_ref[i, :LAT] = (hat * lg).astype(BF)
        hat, _ = layer_stats(feat_ref[i, 256:257].astype(F32))
        first = lax.broadcasted_iota(jnp.int32, (16, D), 0) == 0
        ctx_ref[i, 320:ROWS] = jnp.where(first, hat * fg, 0.0).astype(BF)

    def project(i):
        kv_ref[i, :, :256] = dot(ctx_ref[i], win[1], 1, 0).astype(BF)
        kv_ref[i, :, 256:] = dot(ctx_ref[i], win[2], 1, 0).astype(BF)
        q_ref[i] = by_head(dot(ctx_ref[i, :LAT], win[0], 1, 0), pair).astype(BF)

    def attend(i):
        scores = dot(q_ref[i], kv_ref[i, :, :256], 1, 1) * FACTOR
        scores = jnp.where(live, scores, -1e30)
        shifted = jnp.exp(scores - jnp.max(scores, axis=-1, keepdims=True))
        shifted = jnp.where(live, shifted, 0.0)
        pr_ref[i] = shifted / jnp.sum(shifted, axis=-1, keepdims=True)

    norm(0)
    for c in copies:
        c.wait()
    for i in range(IMGS):
        if i < IMGS - 1:
            norm(i + 1)
        project(i)
        if i > 0:
            attend(i - 1)
    attend(IMGS - 1)


def backward_kernel(owner_ref, sample_ref, a0, a2, kv_ref, q_ref, pr_ref,
                    kvg, g0, g1, g2, lat):
    xh = lax.axis_index("xh")
    co = lax.axis_index("co")
    pair = pair_of(xh, co)
    left = lax.broadcasted_iota(jnp.int32, (ROWS, 128), 1) < 64
    for i in range(IMGS):
        rows = slice(LAT * i, LAT * (i + 1))
        count = scale_of(sample_ref, i).astype(F32)
        total = a0[rows] + a2[rows].astype(F32)
        attn = by_head(total / count, pair).astype(BF)
        probs = pr_ref[i]
        value_grad = dot(probs.astype(BF), attn, 0, 0)
        prob_grad = dot(attn, kv_ref[i, :, 256:], 1, 1)
        inner = jnp.sum(probs * prob_grad, axis=-1, keepdims=True)
        score_grad = (probs * (prob_grad - inner) * FACTOR).astype(BF)
        query_grad = dot(score_grad, kv_ref[i, :, :256], 1, 0)
        query_grad = jnp.where(head_lanes(pair, 0, LAT), query_grad[:LAT],
                               jnp.where(head_lanes(pair, 1, LAT), query_grad[LAT:], 0.0))
        key_grad = dot(score_grad, q_ref[i], 0, 0)
        lat[rows, :256] = query_grad.astype(BF)
        lat[rows, 256:512] = key_grad[:LAT].astype(BF)
        lat[rows, 512:] = value_grad[:LAT].astype(BF)
        at = slice(ROWS * i, ROWS * (i + 1))
        kvg[at, :128] = jnp.where(xh == 0, key_grad[:, :128], key_grad[:, 128:]).astype(BF)
        kvg[at, 128:256] = jnp.where(xh == 0, value_grad[:, :128], value_grad[:, 128:]).astype(BF)
        even = jnp.where(left, key_grad[:, 128:], pltpu.roll(value_grad[:, 128:], 64, 1))
        odd = jnp.where(left, pltpu.roll(key_grad[:, :128], 64, 1), value_grad[:, :128])
        kvg[at, 256:] = jnp.where(xh == 0, even, odd).astype(BF)
    places = (g0, g1.at[:2 * LAT], g2, g1.at[2 * LAT:])
    for out, (dx, dc) in zip(places, AROUND):
        section = (xh ^ dx) * 2 + (co ^ dc)
        for slot in range(2):
            index, _ = slot_image(owner_ref, section, slot)
            out[LAT * slot:LAT * (slot + 1)] = lat[pl.ds(pl.multiple_of(index * LAT, LAT), LAT)]


def weight_kernel(ctx_ref, kvg, w_ref, wide, order):
    ctx = ctx_ref[...].reshape(IMGS * ROWS, D)
    for c in range(5):
        columns = slice(256 * c, 256 * (c + 1))
        wide[columns] = dot(ctx[:, columns], kvg[...], 0, 0)
    for y in range(4):
        for xl in range(2):
            piece = xl * 4 + y
            for z in range(8):
                first = ((z * 4 + y) * 2 + xl) * SHARE
                order[piece, z * SHARE:(z + 1) * SHARE] = wide[first:first + SHARE]
            whole = order[piece]
            keys = whole[:, :128], whole[:, 256:320]
            vals = whole[:, 128:256], whole[:, 320:]
            for k, (main, tail) in enumerate((keys, vals)):
                w_ref[8 * k + piece, 0:160] = main.astype(BF)
                w_ref[8 * k + piece, 160:240] = jnp.concatenate([tail[:80], tail[80:]], axis=1).astype(BF)


def first_sum_kernel(r_ref, out_ref, full, share):
    tails = []
    for k in range(2):
        total = r_ref[8 * k].astype(F32)
        for p in range(1, 8):
            total = total + r_ref[8 * k + p].astype(F32)
        full[:, 256 * k:256 * k + 128] = total[:160]
        tail = total[160:]
        tails.append(jnp.concatenate([tail[:, :64], tail[:, 64:]], axis=0))
    full[:, 128:256] = jnp.concatenate(tails, axis=1)
    for z in range(8):
        for k in range(3):
            share[z, SHARE * k:SHARE * (k + 1)] = full[SHARE * z:SHARE * (z + 1), 128 * k:128 * (k + 1)]
        share[z, 3 * SHARE:] = jnp.zeros((64 - 3 * SHARE, 128), F32)
    out_ref[...] = share[...].astype(BF)


def last_kernel(r_ref, out_ref):
    total = r_ref[0].astype(F32)
    for z in range(1, 8):
        total = total + r_ref[z].astype(F32)
    total = total * (1.0 / 256.0)
    for k in range(3):
        out_ref[:, 128 * k:128 * (k + 1)] = total[SHARE * k:SHARE * (k + 1)]


def near_kernel(owner_ref, part_ref, lat_ref, qw_hbm, kvw_hbm, c1, g0, g1,
                acc_ref, up_ref, hat_ref, inv_ref, far_ref, win, sems):
    xh = lax.axis_index("xh")
    co = lax.axis_index("co")
    copies = []
    for dx, place in ((0, win), (1, far_ref)):
        for dc in range(2):
            start = pl.multiple_of(window_of(pair_of(xh ^ dx, co ^ dc)), 128)
            further = pl.multiple_of(start + INNER, 128)
            for k, (source, lane) in enumerate(((qw_hbm, start), (kvw_hbm, start), (kvw_hbm, further))):
                copies.append(pltpu.make_async_copy(
                    source.at[:, pl.ds(lane, 256)], place.at[3 * dc + k], sems.at[len(copies)]))
    for c in copies:
        c.start()
    for slot in range(2):
        rows = slice(LAT * slot, LAT * (slot + 1))
        index, _ = slot_image(owner_ref, xh * 2 + co, slot)
        up_ref[rows] = part_ref[index].astype(F32) + c1[index].astype(F32)
        hat, inverse = layer_stats(lat_ref[index].astype(F32))
        hat_ref[rows] = hat
        inv_ref[rows] = jnp.broadcast_to(inverse, (LAT, 128))
    total = jnp.zeros((D, 2 * LAT), F32)
    for n in range(6):
        copies[n].wait()
        lanes = slice(256 * (n % 3), 256 * (n % 3 + 1))
        total = total + dot(win[n], (g0, g1)[n // 3][:2 * LAT, lanes], 1, 1)
    acc_ref[...] = total
    for c in copies[6:]:
        c.wait()


def latent_kernel(owner_ref, sample_ref, lg_ref, acc_ref, up_ref, hat_ref, inv_ref, far_ref, u2, g2, out_ref, grad):
    section = lax.axis_index("xh") * 2 + lax.axis_index("co")
    for c in range(5):
        rows = slice(256 * c, 256 * (c + 1))
        block = acc_ref[rows]
        for n in range(6):
            first = 2 * LAT * (n // 3)
            block = block + dot(
                far_ref[n, rows], g2[first:first + 2 * LAT, 256 * (n % 3):256 * (n % 3 + 1)], 1, 1)
        grad[:, rows] = jnp.transpose(block)
    lg = lg_ref[...].reshape(1, D)
    for slot in range(2):
        rows = slice(LAT * slot, LAT * (slot + 1))
        index, found = slot_image(owner_ref, section, slot)
        count = scale_of(sample_ref, index).astype(F32)
        upstream = ((up_ref[rows] + u2[slot].astype(F32)) / count).astype(BF).astype(F32)
        hat = hat_ref[rows]
        dy = grad[rows] * lg
        centred = dy - jnp.mean(dy, axis=-1, keepdims=True) - hat * jnp.mean(dy * hat, axis=-1, keepdims=True)
        out = (upstream + inv_ref[rows, :1] * centred).astype(BF)
        out_ref[slot] = jnp.where(found == 1, out, jnp.zeros_like(out))


SMEM = pl.BlockSpec(memory_space=pltpu.SMEM)
VMEM = pl.BlockSpec(memory_space=pltpu.VMEM)
HBM = pl.BlockSpec(memory_space=pltpu.HBM)
CORE = [(0, 1), (1, 0), (2, 3), (3, 2)]
FAR = [(0, 2), (2, 0), (1, 3), (3, 1)]
DIAGONAL = [(0, 3), (3, 0), (1, 2), (2, 1)]
SECTION = ("xh", "co")


def call(body, name, outs, ins, scratch=(), flops=0, size=0, limit=24):
    return pl.pallas_call(
        body,
        out_shape=outs,
        in_specs=ins,
        out_specs=jax.tree.map(lambda _: VMEM, outs),
        scratch_shapes=list(scratch),
        cost_estimate=pl.CostEstimate(flops=flops, bytes_accessed=size, transcendentals=0),
        compiler_params=pltpu.CompilerParams(vmem_limit_bytes=limit * 2**20),
        name=name,
    )


def swap(x, pairs):
    return lax.ppermute(x, SECTION, pairs)


def bf(*shape):
    return jax.ShapeDtypeStruct(shape, BF)


def wide(*shape):
    return jax.ShapeDtypeStruct(shape, F32)


DMA = pltpu.SemaphoreType.DMA
COST = 1000000
CALLS = dict(
    attn=call(
        attn_kernel, "attn_part", [jax.ShapeDtypeStruct((256, 256), F32), bf(256, 256), bf(2, LAT, D)], [SMEM] + [VMEM] * 4,
        [pltpu.VMEM((IMGS, LAT, D), BF), pltpu.VMEM((256, 384), F32)],
        flops=600_000_000, size=3_000_000),
    forward=call(
        forward_kernel, "forward_part",
        [bf(IMGS, ROWS, D), bf(IMGS, ROWS, 512), bf(IMGS, 2 * LAT, 256),
         jax.ShapeDtypeStruct((IMGS, 2 * LAT, ROWS), F32)],
        [VMEM] * 4 + [HBM] * 2,
        [pltpu.VMEM((3, D, 256), BF), DMA((3,))],
        flops=4_000_000_000, size=12_000_000),
    backward=call(
        backward_kernel, "backward_part",
        [bf(IMGS * ROWS, 384), bf(2 * LAT, 768), bf(4 * LAT, 768), bf(2 * LAT, 768)],
        [SMEM, SMEM] + [VMEM] * 5, [pltpu.VMEM((256, 768), BF)],
        flops=COST, size=1000),
    weight=call(
        weight_kernel, "weight_part", bf(16, 240, 128), [VMEM] * 2,
        [pltpu.VMEM((D, 384), F32), pltpu.VMEM((8, 160, 384), F32)],
        flops=COST, size=1000),
    first=call(first_sum_kernel, "first_sum", bf(8, 64, 128), [VMEM],
               [pltpu.VMEM((160, 384), F32), pltpu.VMEM((8, 64, 128), F32)],
               size=1_000_000),
    last=call(last_kernel, "last_sum", jax.ShapeDtypeStruct((SHARE, 384), F32), [VMEM], size=300_000),
    near=call(
        near_kernel, "near_part", [wide(D, 2 * LAT), wide(2 * LAT, D), wide(2 * LAT, D), wide(2 * LAT, 128),
                                   bf(6, D, 256)],
        [SMEM] + [VMEM] * 2 + [HBM] * 2 + [VMEM] * 3,
        [pltpu.VMEM((6, D, 256), BF), DMA((12,))],
        flops=COST, size=1000, limit=60),
    latent=call(
        latent_kernel, "latent_part", bf(2, LAT, D), [SMEM, SMEM] + [VMEM] * 8,
        [pltpu.VMEM((2 * LAT, D), F32)],
        flops=2_000_000_000, size=9_000_000, limit=60),
)


def per_device(partials, latents, features, feature_gain, latent_gain, query_weight, kv_weight, out_weight,
               sample_of, owner):
    part = partials[0]
    owner = owner.reshape(1, IMGS)
    c1 = swap(part, CORE)
    a0, a2, u = CALLS["attn"](owner, part, c1, out_weight, latents)
    a2 = swap(a2, FAR)
    u = swap(u, FAR)
    ctx, kv, q, probs = CALLS["forward"](
        features, latents, feature_gain, latent_gain, query_weight, kv_weight)
    kvg, g0, g1, g2 = CALLS["backward"](owner, sample_of, a0, a2, kv, q, probs)
    g1 = swap(g1, CORE)
    g2 = jnp.concatenate([g2, g1[2 * LAT:]], axis=0)
    w = CALLS["weight"](ctx, kvg)
    w, u = lax.optimization_barrier((w, u))
    w = lax.all_to_all(w, ("xh", "xl", "y"), 0, 0, tiled=True)
    near = CALLS["near"](owner, part, latents, query_weight, kv_weight, c1, g0, g1)
    g2, near = lax.optimization_barrier((g2, near))
    w, near = lax.optimization_barrier((w, near))
    g2 = swap(g2, FAR)
    w = CALLS["first"](w)
    latent_grad = CALLS["latent"](owner, sample_of, latent_gain, *near, u, g2)
    w = lax.all_to_all(w, "z", 0, 0, tiled=True)
    w, latent_grad = lax.optimization_barrier((w, latent_grad))
    kv_grad = CALLS["last"](w)
    return latent_grad[None], kv_grad


def solution(mesh):
    fine = Mesh(mesh.devices.reshape(2, 2, 8, 4, 2), ("xh", "co", "z", "y", "xl"))
    dp = ("z", "y", "xl")
    return jax.shard_map(
        per_device,
        mesh=fine,
        in_specs=(
            P(SECTION, dp, None, None),
            P(dp, None, None),
            P(dp, None, None),
            P(),
            P(),
            P(),
            P(),
            P(),
            P(dp, None),
            P(dp, None),
        ),
        out_specs=(P(SECTION, dp, None, None), P(dp, SECTION)),
        check_vma=False,
    )
```

```python
import functools
import jax
import jax.numpy as jnp
from jax import lax
from jax.experimental import pallas as pl
from jax.experimental.pallas import tpu as pltpu
from jax.sharding import Mesh, PartitionSpec as P

HEAD = 96
IMGS = 4
LAT = 64
PATCH = 257
TOK = 321
ROWS = 336
D = 1280
INNER = 768
EPS = 1e-05
BF = jnp.bfloat16
F32 = jnp.float32
FACTOR = HEAD ** (-0.5)
SHARE = 20


def dot(a, b, ca, cb):
    return lax.dot_general(a, b, (((ca,), (cb,)), ((), ())), preferred_element_type=F32)


def pair_of(xh, co):
    return co * 2 + xh


def window_of(pair):
    return (pair // 2) * 384 + (pair % 2) * 128


def head_lanes(pair, head, rows):
    lane = lax.broadcasted_iota(jnp.int32, (rows, 256), 1) - ((pair % 2) * 64 + head * HEAD)
    return (lane >= 0) & (lane < HEAD)


def by_head(x, pair):
    zero = jnp.zeros_like(x)
    return jnp.concatenate([jnp.where(head_lanes(pair, h, x.shape[0]), x, zero) for h in range(2)], axis=0)


def layer_stats(x):
    centred = x - jnp.mean(x, axis=-1, keepdims=True)
    inverse = lax.rsqrt(jnp.mean(centred * centred, axis=-1, keepdims=True) + EPS)
    return centred * inverse, inverse


def slot_image(owner_ref, section, slot):
    found = jnp.int32(0)
    index = jnp.int32(0)
    seen = jnp.int32(0)
    for i in range(IMGS):
        mine = (owner_ref[0, i] == section).astype(jnp.int32)
        take = (mine == 1) & (seen == slot)
        index = jnp.where(take, i, index)
        found = jnp.where(take, 1, found)
        seen = seen + mine
    return index, found


def scale_of(sample_ref, i):
    count = jnp.int32(0)
    for k in range(IMGS):
        count = count + (sample_ref[0, k] == sample_ref[0, i]).astype(jnp.int32)
    return count


AROUND = ((0, 0), (0, 1), (1, 0), (1, 1))


def attn_kernel(owner_ref, part_ref, c1_ref, ow_ref, lat_ref, mine, far, u_ref, chip, prod):
    xh = lax.axis_index("xh")
    co = lax.axis_index("co")
    chip[...] = (part_ref[...].astype(F32) + c1_ref[...].astype(F32)).astype(BF)
    group = ow_ref[pl.ds(pl.multiple_of(co * 384, 128), 384)]
    prod[...] = dot(chip[...].reshape(IMGS * LAT, D), group, 1, 1)
    mine[...] = prod[:, pl.ds(pl.multiple_of(xh * 128, 128), 256)]
    far[...] = prod[:, pl.ds(pl.multiple_of((1 - xh) * 128, 128), 256)].astype(BF)
    for slot in range(2):
        index, _ = slot_image(owner_ref, (xh ^ 1) * 2 + co, slot)
        u_ref[slot] = chip[index]


def forward_kernel(feat_ref, lat_ref, fg_ref, lg_ref, qw_hbm, kvw_hbm, ctx_ref, kv_ref, q_ref, pr_ref, win, sems):
    pair = pair_of(lax.axis_index("xh"), lax.axis_index("co"))
    start = pl.multiple_of(window_of(pair), 128)
    copies = [
        pltpu.make_async_copy(qw_hbm.at[:, pl.ds(start, 256)], win.at[0], sems.at[0]),
        pltpu.make_async_copy(kvw_hbm.at[:, pl.ds(start, 256)], win.at[1], sems.at[1]),
        pltpu.make_async_copy(kvw_hbm.at[:, pl.ds(pl.multiple_of(start + INNER, 128), 256)], win.at[2], sems.at[2]),
    ]
    for c in copies:
        c.start()
    fg = fg_ref[...].reshape(1, D)
    lg = lg_ref[...].reshape(1, D)
    live = lax.broadcasted_iota(jnp.int32, (2 * LAT, ROWS), 1) < TOK

    def norm(i):
        for c in range(4):
            hat, _ = layer_stats(feat_ref[i, 64 * c:64 * (c + 1)].astype(F32))
            ctx_ref[i, LAT + 64 * c:LAT + 64 * (c + 1)] = (hat * fg).astype(BF)
        hat, _ = layer_stats(lat_ref[i].astype(F32))
        ctx_ref[i, :LAT] = (hat * lg).astype(BF)
        hat, _ = layer_stats(feat_ref[i, 256:257].astype(F32))
        first = lax.broadcasted_iota(jnp.int32, (16, D), 0) == 0
        ctx_ref[i, 320:ROWS] = jnp.where(first, hat * fg, 0.0).astype(BF)

    def project(i):
        kv_ref[i, :, :256] = dot(ctx_ref[i], win[1], 1, 0).astype(BF)
        kv_ref[i, :, 256:] = dot(ctx_ref[i], win[2], 1, 0).astype(BF)
        q_ref[i] = by_head(dot(ctx_ref[i, :LAT], win[0], 1, 0), pair).astype(BF)

    def attend(i):
        scores = dot(q_ref[i], kv_ref[i, :, :256], 1, 1) * FACTOR
        scores = jnp.where(live, scores, -1e30)
        shifted = jnp.exp(scores - jnp.max(scores, axis=-1, keepdims=True))
        shifted = jnp.where(live, shifted, 0.0)
        pr_ref[i] = shifted / jnp.sum(shifted, axis=-1, keepdims=True)

    norm(0)
    for c in copies:
        c.wait()
    for i in range(IMGS):
        if i < IMGS - 1:
            norm(i + 1)
        project(i)
        if i > 0:
            attend(i - 1)
    attend(IMGS - 1)


def backward_kernel(owner_ref, sample_ref, a0, a2, kv_ref, q_ref, pr_ref,
                    kvg, g0, g1, g2, lat):
    xh = lax.axis_index("xh")
    co = lax.axis_index("co")
    pair = pair_of(xh, co)
    left = lax.broadcasted_iota(jnp.int32, (ROWS, 128), 1) < 64
    for i in range(IMGS):
        rows = slice(LAT * i, LAT * (i + 1))
        count = scale_of(sample_ref, i).astype(F32)
        total = a0[rows] + a2[rows].astype(F32)
        attn = by_head(total / count, pair).astype(BF)
        probs = pr_ref[i]
        value_grad = dot(probs.astype(BF), attn, 0, 0)
        prob_grad = dot(attn, kv_ref[i, :, 256:], 1, 1)
        inner = jnp.sum(probs * prob_grad, axis=-1, keepdims=True)
        score_grad = (probs * (prob_grad - inner) * FACTOR).astype(BF)
        query_grad = dot(score_grad, kv_ref[i, :, :256], 1, 0)
        query_grad = jnp.where(head_lanes(pair, 0, LAT), query_grad[:LAT],
                               jnp.where(head_lanes(pair, 1, LAT), query_grad[LAT:], 0.0))
        key_grad = dot(score_grad, q_ref[i], 0, 0)
        lat[rows, :256] = query_grad.astype(BF)
        lat[rows, 256:512] = key_grad[:LAT].astype(BF)
        lat[rows, 512:] = value_grad[:LAT].astype(BF)
        at = slice(ROWS * i, ROWS * (i + 1))
        kvg[at, :128] = jnp.where(xh == 0, key_grad[:, :128], key_grad[:, 128:]).astype(BF)
        kvg[at, 128:256] = jnp.where(xh == 0, value_grad[:, :128], value_grad[:, 128:]).astype(BF)
        even = jnp.where(left, key_grad[:, 128:], pltpu.roll(value_grad[:, 128:], 64, 1))
        odd = jnp.where(left, pltpu.roll(key_grad[:, :128], 64, 1), value_grad[:, :128])
        kvg[at, 256:] = jnp.where(xh == 0, even, odd).astype(BF)
    places = (g0, g1.at[:2 * LAT], g2, g1.at[2 * LAT:])
    for out, (dx, dc) in zip(places, AROUND):
        section = (xh ^ dx) * 2 + (co ^ dc)
        for slot in range(2):
            index, _ = slot_image(owner_ref, section, slot)
            out[LAT * slot:LAT * (slot + 1)] = lat[pl.ds(pl.multiple_of(index * LAT, LAT), LAT)]


def weight_kernel(ctx_ref, kvg, w_hbm, wide, order, w_ref, sems):
    ctx = ctx_ref[...].reshape(IMGS * ROWS, D)
    for c in range(5):
        columns = slice(256 * c, 256 * (c + 1))
        wide[columns] = dot(ctx[:, columns], kvg[...], 0, 0)
    copies = []
    for y in range(4):
        for xl in range(2):
            piece = xl * 4 + y
            for z in range(8):
                first = ((z * 4 + y) * 2 + xl) * SHARE
                order[piece, z * SHARE:(z + 1) * SHARE] = wide[first:first + SHARE]
            whole = order[piece]
            keys = whole[:, :128], whole[:, 256:320]
            vals = whole[:, 128:256], whole[:, 320:]
            for k, (main, tail) in enumerate((keys, vals)):
                w_ref[8 * k + piece, 0:160] = main.astype(BF)
                at = 8 * k + piece
                w_ref[at, 160:240] = jnp.concatenate([tail[:80], tail[80:]], axis=1).astype(BF)
                copies.append(pltpu.make_async_copy(w_ref.at[at], w_hbm.at[at], sems.at[at]))
                copies[-1].start()
    for c in copies:
        c.wait()


def first_sum_kernel(r_ref, out_ref, full, share):
    tails = []
    for k in range(2):
        total = r_ref[8 * k].astype(F32)
        for p in range(1, 8):
            total = total + r_ref[8 * k + p].astype(F32)
        full[:, 256 * k:256 * k + 128] = total[:160]
        tail = total[160:]
        tails.append(jnp.concatenate([tail[:, :64], tail[:, 64:]], axis=0))
    full[:, 128:256] = jnp.concatenate(tails, axis=1)
    for z in range(8):
        for k in range(3):
            share[z, SHARE * k:SHARE * (k + 1)] = full[SHARE * z:SHARE * (z + 1), 128 * k:128 * (k + 1)]
        share[z, 3 * SHARE:] = jnp.zeros((64 - 3 * SHARE, 128), F32)
    out_ref[...] = share[...].astype(BF)


def last_kernel(r_ref, out_ref):
    total = r_ref[0].astype(F32)
    for z in range(1, 8):
        total = total + r_ref[z].astype(F32)
    total = total * (1.0 / 256.0)
    for k in range(3):
        out_ref[:, 128 * k:128 * (k + 1)] = total[SHARE * k:SHARE * (k + 1)]


def near_kernel(owner_ref, part_ref, lat_ref, qw_hbm, kvw_hbm, c1, g0, g1,
                acc_ref, up_ref, hat_ref, inv_ref, far_ref, win, sems):
    xh = lax.axis_index("xh")
    co = lax.axis_index("co")
    copies = []
    for dx, place in ((0, win), (1, far_ref)):
        for dc in range(2):
            start = pl.multiple_of(window_of(pair_of(xh ^ dx, co ^ dc)), 128)
            further = pl.multiple_of(start + INNER, 128)
            for k, (source, lane) in enumerate(((qw_hbm, start), (kvw_hbm, start), (kvw_hbm, further))):
                copies.append(pltpu.make_async_copy(
                    source.at[:, pl.ds(lane, 256)], place.at[3 * dc + k], sems.at[len(copies)]))
    for c in copies:
        c.start()
    for slot in range(2):
        rows = slice(LAT * slot, LAT * (slot + 1))
        index, _ = slot_image(owner_ref, xh * 2 + co, slot)
        up_ref[rows] = part_ref[index].astype(F32) + c1[index].astype(F32)
        hat, inverse = layer_stats(lat_ref[index].astype(F32))
        hat_ref[rows] = hat
        inv_ref[rows] = jnp.broadcast_to(inverse, (LAT, 128))
    total = jnp.zeros((D, 2 * LAT), F32)
    for n in range(6):
        copies[n].wait()
        lanes = slice(256 * (n % 3), 256 * (n % 3 + 1))
        total = total + dot(win[n], (g0, g1)[n // 3][:2 * LAT, lanes], 1, 1)
    acc_ref[...] = total
    for c in copies[6:]:
        c.wait()


def latent_kernel(owner_ref, sample_ref, lg_ref, acc_ref, up_ref, hat_ref, inv_ref, far_ref, u2, g2, out_ref, grad):
    section = lax.axis_index("xh") * 2 + lax.axis_index("co")
    for c in range(5):
        rows = slice(256 * c, 256 * (c + 1))
        block = acc_ref[rows]
        for n in range(6):
            first = 2 * LAT * (n // 3)
            block = block + dot(
                far_ref[n, rows], g2[first:first + 2 * LAT, 256 * (n % 3):256 * (n % 3 + 1)], 1, 1)
        grad[:, rows] = jnp.transpose(block)
    lg = lg_ref[...].reshape(1, D)
    for slot in range(2):
        rows = slice(LAT * slot, LAT * (slot + 1))
        index, found = slot_image(owner_ref, section, slot)
        count = scale_of(sample_ref, index).astype(F32)
        upstream = ((up_ref[rows] + u2[slot].astype(F32)) / count).astype(BF).astype(F32)
        hat = hat_ref[rows]
        dy = grad[rows] * lg
        centred = dy - jnp.mean(dy, axis=-1, keepdims=True) - hat * jnp.mean(dy * hat, axis=-1, keepdims=True)
        out = (upstream + inv_ref[rows, :1] * centred).astype(BF)
        out_ref[slot] = jnp.where(found == 1, out, jnp.zeros_like(out))


SMEM = pl.BlockSpec(memory_space=pltpu.SMEM)
VMEM = pl.BlockSpec(memory_space=pltpu.VMEM)
HBM = pl.BlockSpec(memory_space=pltpu.HBM)
CORE = [(0, 1), (1, 0), (2, 3), (3, 2)]
FAR = [(0, 2), (2, 0), (1, 3), (3, 1)]
DIAGONAL = [(0, 3), (3, 0), (1, 2), (2, 1)]
SECTION = ("xh", "co")


def call(body, name, outs, ins, scratch=(), flops=0, size=0, limit=24, place=VMEM):
    return pl.pallas_call(
        body,
        out_shape=outs,
        in_specs=ins,
        out_specs=jax.tree.map(lambda _: place, outs),
        scratch_shapes=list(scratch),
        cost_estimate=pl.CostEstimate(flops=flops, bytes_accessed=size, transcendentals=0),
        compiler_params=pltpu.CompilerParams(vmem_limit_bytes=limit * 2**20),
        name=name,
    )


def swap(x, pairs):
    return lax.ppermute(x, SECTION, pairs)


def bf(*shape):
    return jax.ShapeDtypeStruct(shape, BF)


def wide(*shape):
    return jax.ShapeDtypeStruct(shape, F32)


DMA = pltpu.SemaphoreType.DMA
COST = 1000000
CALLS = dict(
    attn=call(
        attn_kernel, "attn_part", [jax.ShapeDtypeStruct((256, 256), F32), bf(256, 256), bf(2, LAT, D)], [SMEM] + [VMEM] * 4,
        [pltpu.VMEM((IMGS, LAT, D), BF), pltpu.VMEM((256, 384), F32)],
        flops=600_000_000, size=3_000_000),
    forward=call(
        forward_kernel, "forward_part",
        [bf(IMGS, ROWS, D), bf(IMGS, ROWS, 512), bf(IMGS, 2 * LAT, 256),
         jax.ShapeDtypeStruct((IMGS, 2 * LAT, ROWS), F32)],
        [VMEM] * 4 + [HBM] * 2,
        [pltpu.VMEM((3, D, 256), BF), DMA((3,))],
        flops=4_000_000_000, size=12_000_000),
    backward=call(
        backward_kernel, "backward_part",
        [bf(IMGS * ROWS, 384), bf(2 * LAT, 768), bf(4 * LAT, 768), bf(2 * LAT, 768)],
        [SMEM, SMEM] + [VMEM] * 5, [pltpu.VMEM((256, 768), BF)],
        flops=COST, size=1000),
    weight=call(
        weight_kernel, "weight_part", bf(16, 240, 128), [VMEM] * 2,
        [pltpu.VMEM((D, 384), F32), pltpu.VMEM((8, 160, 384), F32), pltpu.VMEM((16, 240, 128), BF), DMA((16,))],
        place=HBM,
        flops=COST, size=1000),
    first=call(first_sum_kernel, "first_sum", bf(8, 64, 128), [VMEM],
               [pltpu.VMEM((160, 384), F32), pltpu.VMEM((8, 64, 128), F32)],
               size=1_000_000),
    last=call(last_kernel, "last_sum", jax.ShapeDtypeStruct((SHARE, 384), F32), [VMEM], size=300_000),
    near=call(
        near_kernel, "near_part", [wide(D, 2 * LAT), wide(2 * LAT, D), wide(2 * LAT, D), wide(2 * LAT, 128),
                                   bf(6, D, 256)],
        [SMEM] + [VMEM] * 2 + [HBM] * 2 + [VMEM] * 3,
        [pltpu.VMEM((6, D, 256), BF), DMA((12,))],
        flops=COST, size=1000, limit=60),
    latent=call(
        latent_kernel, "latent_part", bf(2, LAT, D), [SMEM, SMEM] + [VMEM] * 8,
        [pltpu.VMEM((2 * LAT, D), F32)],
        flops=2_000_000_000, size=9_000_000, limit=60),
)


def per_device(partials, latents, features, feature_gain, latent_gain, query_weight, kv_weight, out_weight,
               sample_of, owner):
    part = partials[0]
    owner = owner.reshape(1, IMGS)
    c1 = swap(part, CORE)
    a0, a2, u = CALLS["attn"](owner, part, c1, out_weight, latents)
    a2 = swap(a2, FAR)
    u = swap(u, FAR)
    ctx, kv, q, probs = CALLS["forward"](
        features, latents, feature_gain, latent_gain, query_weight, kv_weight)
    kvg, g0, g1, g2 = CALLS["backward"](owner, sample_of, a0, a2, kv, q, probs)
    g1 = swap(g1, CORE)
    g2 = jnp.concatenate([g2, g1[2 * LAT:]], axis=0)
    w = CALLS["weight"](ctx, kvg)
    w, u = lax.optimization_barrier((w, u))
    w = lax.all_to_all(w, ("xh", "xl", "y"), 0, 0, tiled=True)
    near = CALLS["near"](owner, part, latents, query_weight, kv_weight, c1, g0, g1)
    g2, near = lax.optimization_barrier((g2, near))
    w, near = lax.optimization_barrier((w, near))
    g2 = swap(g2, FAR)
    w = CALLS["first"](w)
    latent_grad = CALLS["latent"](owner, sample_of, latent_gain, *near, u, g2)
    w = lax.all_to_all(w, "z", 0, 0, tiled=True)
    w, latent_grad = lax.optimization_barrier((w, latent_grad))
    kv_grad = CALLS["last"](w)
    return latent_grad[None], kv_grad


def solution(mesh):
    fine = Mesh(mesh.devices.reshape(2, 2, 8, 4, 2), ("xh", "co", "z", "y", "xl"))
    dp = ("z", "y", "xl")
    return jax.shard_map(
        per_device,
        mesh=fine,
        in_specs=(
            P(SECTION, dp, None, None),
            P(dp, None, None),
            P(dp, None, None),
            P(),
            P(),
            P(),
            P(),
            P(),
            P(dp, None),
            P(dp, None),
        ),
        out_specs=(P(SECTION, dp, None, None), P(dp, SECTION)),
        check_vma=False,
    )
```
